256 devices in a mesh: row: 16 (over y_lo, z), col: 16 (over x, y_hi, core).
Axes of the slice: x: 4, y: 4 (y_hi: 2, y_lo: 2; y = y_hi * 2 + y_lo), z: 8, core: 2. Of those that a mesh axis runs over, the one named last changes fastest.
Arguments:
- pair_act: bfloat16 [512, 512, 128], P('row', 'col'), may hold values from -6 to 6
- residue_mask: int32 [512], replicated, may hold values 0 or 1
- outgoing_weights: bfloat16 [128, 640], replicated, may hold values from -0.5 to 0.5
- outgoing_final: bfloat16 [128, 128], replicated, may hold values from -0.5 to 0.5
- incoming_weights: bfloat16 [128, 640], replicated, may hold values from -0.5 to 0.5
- incoming_final: bfloat16 [128, 128], replicated, may hold values from -0.5 to 0.5
Outputs:
- pair_out: bfloat16 [512, 512, 128], P('row', 'col')
The draws below stay inside these ranges and needn't reach their ends.
All inputs are finite; a program needn't handle non-finite values.
Results may differ from the reference program's by a relative error of at most 0.015.
Values may be sent and summed in bfloat16 or wider, within the bound.
A program may use at most 128 MiB of HBM per device.

```python
import jax
import jax.numpy as jnp
from jax import lax

C = 128
H = 128
RES = 512


def with_ends(values, key, smallest, high):
    dims = values.shape
    index_at = [jax.random.randint(jax.random.fold_in(key, axis), (), 0, dims[axis]) for axis in range(len(dims))]
    values = values.at[tuple(index_at)].set(smallest)
    longest = dims.index(max(dims))
    index_at[longest] = (index_at[longest] + 1) % dims[longest]
    return values.at[tuple(index_at)].set(high)


def level_of(key, extent, split, least, largest):
    factor_of, own = 1.0, jax.random.fold_in(key, 6)
    for position, shards_of in split:
        steps = jnp.exp(jax.random.uniform(jax.random.fold_in(own, position), (shards_of,), jnp.float32, least / len(split), largest / len(split)))
        factor_of = factor_of * jnp.repeat(steps, extent[position] // shards_of).reshape([-1 if axis == position else 1 for axis in range(len(extent))])
    return factor_of


def gaussian(own_key, shape, scale, reach, split=(), kind=jnp.bfloat16):
    level = level_of(own_key, shape, split, -0.22, 0.18) if split else 1.0
    result = jax.random.normal(own_key, shape, jnp.float32) * scale * level
    return jnp.minimum(jnp.maximum(result, -reach), reach).astype(kind)


def setup_inputs(seed: int = 0) -> dict:
    seeds = jax.random.split(jax.random.key(seed), 7)
    pair_act = gaussian(seeds[0], (RES, RES, C), 1.0, 6.0, ((0, 16), (1, 16)))
    residue_mask = with_ends((jax.random.randint(seeds[1], (RES,), 0, 8) < 7).astype(jnp.int32), jax.random.fold_in(seeds[1], 1), 0, 1)
    outgoing_weights = gaussian(seeds[2], (C, 4 * H + C), C ** -0.5, 0.5)
    outgoing_final = gaussian(seeds[3], (H, C), H ** -0.5, 0.5)
    incoming_weights = gaussian(seeds[4], (C, 4 * H + C), C ** -0.5, 0.5)
    incoming_final = gaussian(seeds[5], (H, C), H ** -0.5, 0.5)
    return dict(pair_act=pair_act, residue_mask=residue_mask, outgoing_weights=outgoing_weights, outgoing_final=outgoing_final, incoming_weights=incoming_weights, incoming_final=incoming_final)


def layer_norm(values):
    middle = lax.optimization_barrier(jnp.mean(values, axis=-1, keepdims=True))
    centred = values - middle
    spread = lax.optimization_barrier(jnp.mean(centred * centred, axis=-1, keepdims=True))
    return centred * lax.rsqrt(spread + 1e-05)

def triangle(pair_act, residue_mask, weights, final, outgoing):
    normed = layer_norm(pair_act.astype(jnp.float32)).astype(jnp.bfloat16)
    valid = residue_mask.astype(jnp.float32)
    pair_mask = (valid[:, None] * valid[None, :])[..., None]
    mixed = jnp.dot(normed.reshape(-1, C), weights, preferred_element_type=jnp.float32).reshape(RES, RES, 4 * H + C)
    left = (pair_mask * jax.nn.sigmoid(mixed[..., H:2 * H]) * mixed[..., :H]).astype(jnp.bfloat16)
    right = (pair_mask * jax.nn.sigmoid(mixed[..., 3 * H:4 * H]) * mixed[..., 2 * H:3 * H]).astype(jnp.bfloat16)
    gate_values = jax.nn.sigmoid(mixed[..., 4 * H:])
    if outgoing:
        summed = jnp.einsum('ikh,jkh->ijh', left.astype(jnp.float32), right.astype(jnp.float32))
    else:
        summed = jnp.einsum('kih,kjh->ijh', left.astype(jnp.float32), right.astype(jnp.float32))
    hidden = layer_norm(summed).astype(jnp.bfloat16)
    update = jnp.dot(hidden.reshape(-1, H), final, preferred_element_type=jnp.float32).reshape(RES, RES, C)
    return (pair_act.astype(jnp.float32) + gate_values * update).astype(jnp.bfloat16)

def reference(pair_act, residue_mask, outgoing_weights, outgoing_final, incoming_weights, incoming_final):
    middle_pair = triangle(pair_act, residue_mask, outgoing_weights, outgoing_final, True)
    return triangle(middle_pair, residue_mask, incoming_weights, incoming_final, False)
```

```python
import jax
import jax.numpy as jnp
from jax import lax
from jax.sharding import PartitionSpec as P


def layer_norm(values, axis):
    middle = jnp.mean(values, axis=axis, keepdims=True)
    centred = values - middle
    spread = jnp.mean(centred * centred, axis=axis, keepdims=True)
    return centred * lax.rsqrt(spread + 1e-05)


def triangle(pair, pair_mask, weights, final, outgoing):
    n, m, channels = pair.shape
    width = final.shape[0]
    rows, cols = lax.axis_size("row"), lax.axis_size("col")
    group = width // rows
    normed = layer_norm(pair.astype(jnp.float32), -1).astype(jnp.bfloat16)
    mixed = jnp.einsum(
        "cw,ikc->wik", weights, normed, preferred_element_type=jnp.float32
    )
    part = mixed[: 4 * width].reshape(2, 2, width, n, m)
    sides = (pair_mask * jax.nn.sigmoid(part[:, 1]) * part[:, 0]).astype(jnp.bfloat16)
    gate = jax.nn.sigmoid(mixed[4 * width :])
    sides = sides.reshape(2, rows, group, n, m).transpose(1, 2, 0, 3, 4)
    sides = lax.all_to_all(sides, "row", 0, 0, tiled=True)
    sides = sides.transpose(1, 0, 2, 3, 4)
    sides = jnp.repeat(sides, cols // group, axis=0)
    sides = lax.all_to_all(sides, "col", 0, 0, tiled=True)
    sides = sides.reshape(cols, rows, 2, n, m)
    left, right = sides[:, :, 0], sides[:, :, 1]
    half = lax.axis_index("col") % 2
    if outgoing:
        left = lax.dynamic_slice_in_dim(left, half * (rows // 2), rows // 2, 1)
        left = left.transpose(1, 2, 0, 3).reshape(rows * n // 2, cols * m)
        right = right.transpose(1, 2, 0, 3).reshape(rows * n, cols * m)
        summed = lax.dot_general(
            left, right, (((1,), (1,)), ((), ())), preferred_element_type=jnp.float32
        )
    else:
        left = lax.dynamic_slice_in_dim(left, half * (cols // 2), cols // 2, 0)
        left = left.transpose(1, 2, 0, 3).reshape(rows * n, cols * m // 2)
        right = right.transpose(1, 2, 0, 3).reshape(rows * n, cols * m)
        summed = lax.dot_general(
            left, right, (((0,), (0,)), ((), ())), preferred_element_type=jnp.float32
        )
    summed = summed.astype(jnp.bfloat16).reshape(rows * n // 2, cols, m).transpose(1, 0, 2)
    summed = lax.all_to_all(summed, "col", 0, 0, tiled=True)
    summed = summed.reshape(group, rows, n, m).transpose(1, 0, 2, 3)
    summed = lax.all_to_all(summed, "row", 0, 0, tiled=True)
    summed = summed.reshape(width, n * m)
    hidden = layer_norm(summed.astype(jnp.float32), 0).astype(jnp.bfloat16)
    update = lax.dot_general(
        final, hidden, (((0,), (0,)), ((), ())), preferred_element_type=jnp.float32
    )
    update = (gate.reshape(channels, n * m) * update).T.reshape(n, m, channels)
    return (pair.astype(jnp.float32) + update).astype(jnp.bfloat16)


def shards(
    pair_act, residue_mask, outgoing_weights, outgoing_final, incoming_weights, incoming_final
):
    n, m, _ = pair_act.shape
    valid = residue_mask.astype(jnp.float32)
    valid_rows = lax.dynamic_slice_in_dim(valid, lax.axis_index("row") * n, n, 0)
    valid_cols = lax.dynamic_slice_in_dim(valid, lax.axis_index("col") * m, m, 0)
    pair_mask = valid_rows[:, None] * valid_cols[None, :]
    middle = triangle(pair_act, pair_mask, outgoing_weights, outgoing_final, True)
    return triangle(middle, pair_mask, incoming_weights, incoming_final, False)


def solution(mesh):
    return jax.shard_map(
        shards,
        mesh=mesh,
        in_specs=(P("row", "col", None), P(), P(), P(), P(), P()),
        out_specs=P("row", "col", None),
        check_vma=False,
    )
```

```python
import functools

import jax
import jax.numpy as jnp
from jax import lax
from jax.experimental import pallas as pl
from jax.experimental.pallas import tpu as pltpu
from jax.sharding import PartitionSpec as P

ROWS = 16
COLS = 16
CH = 128
BLK = 32
SUB = 8
CHUNKS = 4
PER = ROWS // CHUNKS


def block_transpose(parts):
    lane = lax.broadcasted_iota(jnp.int32, parts[0].shape, 1)
    low = lane < 64
    even = (lane // 32) % 2 == 0
    t0, t1, t2, t3 = parts
    u0 = jnp.where(low, t0, pltpu.roll(t2, 64, 1))
    u2 = jnp.where(low, pltpu.roll(t0, 64, 1), t2)
    u1 = jnp.where(low, t1, pltpu.roll(t3, 64, 1))
    u3 = jnp.where(low, pltpu.roll(t1, 64, 1), t3)
    return (
        jnp.where(even, u0, pltpu.roll(u1, 32, 1)),
        jnp.where(even, pltpu.roll(u0, 96, 1), u1),
        jnp.where(even, u2, pltpu.roll(u3, 32, 1)),
        jnp.where(even, pltpu.roll(u2, 96, 1), u3),
    )


def kernel(
    mask_ref, pair_ref, w_out, f_out, w_in, f_in, out_ref,
    pair_t, weights_t, final_t, half_mask, normed, mixed, gate, stage,
    send1, recv1, recv2, left_o, left_i, right, summed, send3, recv3, send4, recv4,
    hidden, hidden_t,
    s1, r1, s2, r2, s3, r3, s4, r4,
):
    row, col = lax.axis_index("row"), lax.axis_index("col")
    y_lo, z = row // 8, row % 8
    x, y_hi, core = col // 4, (col // 2) % 2, col % 2
    chip = col // 2

    def z_step(b):
        return ((b + 1) // 2) * (2 * (b % 2) - 1)

    def row_to(d):
        return ((y_lo + d % 2) % 2) * 8 + (z + z_step(d // 2) + 8) % 8

    def row_from(d):
        return ((y_lo + d % 2) % 2) * 8 + (z - z_step(d // 2) + 8) % 8

    def col_to(e):
        return ((x + e // 4) % 4) * 4 + ((y_hi + (e // 2) % 2) % 2) * 2 + (core + e % 2) % 2

    def col_from(e):
        return ((x + 4 - e // 4) % 4) * 4 + ((y_hi + (e // 2) % 2) % 2) * 2 + (core + e % 2) % 2

    barrier = pltpu.get_barrier_semaphore()

    @pl.loop(1, 16)
    def _(d):
        pl.semaphore_signal(barrier, inc=1, device_id={"row": row_to(d)}, device_id_type=pl.DeviceIdType.MESH)
        pl.semaphore_signal(barrier, inc=1, device_id={"col": col_to(d)}, device_id_type=pl.DeviceIdType.MESH)

    for s in range(SUB):
        block = jnp.concatenate([pair_ref[8 * q + s] for q in range(4)], axis=0)
        pair_t[:, s * 128 : (s + 1) * 128] = block.astype(jnp.float32).T
    for u, (w, f) in enumerate(((w_out, f_out), (w_in, f_in))):
        weights_t[u] = w[...].astype(jnp.float32).T.astype(jnp.bfloat16)
        final_t[u] = f[...].astype(jnp.float32).T.astype(jnp.bfloat16)

    lane = lax.broadcasted_iota(jnp.int32, (SUB, 128), 1)
    sub = lax.broadcasted_iota(jnp.int32, (SUB, 128), 0)
    by_row = jnp.zeros((SUB, 128), jnp.float32)
    by_col = jnp.zeros((SUB, 128), jnp.float32)
    for k in range(BLK):
        by_col = jnp.where(lane % 32 == k, mask_ref[col * BLK + k].astype(jnp.float32), by_col)
        by_row = jnp.where(
            (lane // 32) * 8 + sub == k, mask_ref[row * BLK + k].astype(jnp.float32), by_row
        )
    half_mask[...] = 0.5 * by_row * by_col

    def row_copy(src, dst, ssem, rsem, d):
        return pltpu.make_async_remote_copy(
            src_ref=src, dst_ref=dst, send_sem=ssem, recv_sem=rsem,
            device_id={"row": row_to(d)}, device_id_type=pl.DeviceIdType.MESH,
        )

    def col_copy(src, dst, ssem, rsem, e):
        return pltpu.make_async_remote_copy(
            src_ref=src, dst_ref=dst, send_sem=ssem, recv_sem=rsem,
            device_id={"col": col_to(e)}, device_id_type=pl.DeviceIdType.MESH,
        )

    def copy1(u, d):
        return row_copy(send1.at[u, d], recv1.at[u, d], s1.at[u, d], r1.at[u, d], d)

    def copy2(u, g, e):
        there = col_to(e) // 2
        return col_copy(
            recv1.at[u, pl.ds(g * PER, PER), there], recv2.at[u, col, pl.ds(g * PER, PER)],
            s2.at[u, g, e], r2.at[u, g, e], e,
        )

    def copy3(u, e):
        return col_copy(send3.at[u, col_to(e)], recv3.at[u, col], s3.at[u, e], r3.at[u, e], e)

    def copy4(u, d):
        return row_copy(send4.at[u, row_to(d)], recv4.at[u, row], s4.at[u, d], r4.at[u, d], d)

    def project(u):
        for j in range(4):
            cols = slice(256 * j, 256 * (j + 1))
            values = pair_t[:, cols]
            middle = jnp.mean(values, axis=0, keepdims=True)
            centred = values - middle
            spread = jnp.mean(centred * centred, axis=0, keepdims=True)
            normed[:, cols] = (centred * lax.rsqrt(spread + 1e-05)).astype(jnp.bfloat16)
            mixed[:, cols] = jnp.dot(
                weights_t[u], normed[:, cols], preferred_element_type=jnp.float32
            )

    def sides(u, d):
        at = row_to(d) * 8

        def part(k):
            return mixed[pl.ds(pl.multiple_of(at + k * CH, 8), 8), :]

        for side in range(2):
            value, gates = part(2 * side), part(2 * side + 1)
            for s in range(SUB):
                cols = slice(s * 128, (s + 1) * 128)
                stage[pl.ds(side * 8 + s, 8, stride=16), :] = (
                    (jnp.tanh(0.5 * gates[:, cols]) + 1.0) * value[:, cols] * half_mask[s : s + 1, :]
                )
        return stage[...].astype(jnp.bfloat16).reshape(8, 16, 128)

    def assemble_right(u, g):
        for cc in range(4):
            tiles = [
                recv2[u, 4 * cc + t, pl.ds(g * PER, PER)].astype(jnp.float32)[:, 8:].reshape(PER * 8, 128)
                for t in range(4)
            ]
            turned = block_transpose(tiles)
            for i in range(PER):
                rows = jnp.concatenate([v[8 * i : 8 * i + 8] for v in turned], axis=0)
                at = pl.multiple_of(row_from(g * PER + i) * BLK, BLK)
                right[pl.ds(at, BLK), cc * 128 : (cc + 1) * 128] = rows.astype(jnp.bfloat16)

    def assemble_left_o(u, g):
        a = (core + y_lo) % 2
        for cc in range(4):
            tiles = [
                jnp.concatenate(
                    [recv2[u, 4 * cc + t, g * PER + 2 * i + a].astype(jnp.float32)[:8] for i in range(PER // 2)],
                    axis=0,
                )
                for t in range(4)
            ]
            turned = block_transpose(tiles)
            for i in range(PER // 2):
                rows = jnp.concatenate([v[8 * i : 8 * i + 8] for v in turned], axis=0)
                at = pl.multiple_of((row_from(g * PER + 2 * i) % 8) * BLK, BLK)
                left_o[pl.ds(at, BLK), cc * 128 : (cc + 1) * 128] = rows.astype(jnp.bfloat16)

    def assemble_left_i(u, g):
        for cc in range(2):
            tiles = [
                recv2[u, (2 * core + cc) * 4 + t, pl.ds(g * PER, PER)]
                .astype(jnp.float32)[:, :8]
                .reshape(PER * 8, 128)
                for t in range(4)
            ]
            turned = block_transpose(tiles)
            for i in range(PER):
                rows = jnp.concatenate([v[8 * i : 8 * i + 8] for v in turned], axis=0)
                at = pl.multiple_of(row_from(g * PER + i) * BLK, BLK)
                left_i[pl.ds(at, BLK), cc * 128 : (cc + 1) * 128] = rows.astype(jnp.bfloat16)

    for u in range(2):
        project(u)
        if u == 0:
            pl.semaphore_wait(barrier, 30)

        recv1[u, 0] = sides(u, 0)

        @pl.loop(1, ROWS)
        def _(d):
            send1[u, d] = sides(u, d)
            copy1(u, d).start()

        gate[...] = 0.5 * jnp.tanh(0.5 * mixed[4 * CH :, :]) + 0.5

        @pl.loop(0, CHUNKS)
        def _(g):
            @pl.loop(g * PER, (g + 1) * PER)
            def _(d):
                @pl.when(d > 0)
                def _():
                    copy1(u, d).wait_recv()

            @pl.loop(1, COLS)
            def _(e):
                copy2(u, g, e).start()

            recv2[u, col, pl.ds(g * PER, PER)] = recv1[u, pl.ds(g * PER, PER), chip]

        @pl.loop(0, CHUNKS)
        def _(g):
            @pl.loop(1, COLS)
            def _(e):
                copy2(u, g, e).wait_recv()

            assemble_right(u, g)
            if u == 0:
                assemble_left_o(u, g)
            else:
                assemble_left_i(u, g)

        if u == 0:
            summed[...] = lax.dot_general(
                left_o[...], right[...], (((1,), (1,)), ((), ())), preferred_element_type=jnp.float32
            )
        else:
            summed[...] = lax.dot_general(
                left_i[...], right[...], (((0,), (0,)), ((), ())), preferred_element_type=jnp.float32
            )

        for pair in range(4):
            for cc in range(4):
                parts = [
                    jnp.concatenate(
                        [
                            summed[64 * pair + 32 * i + 8 * q : 64 * pair + 32 * i + 8 * q + 8, cc * 128 : (cc + 1) * 128]
                            for i in range(2)
                        ],
                        axis=0,
                    )
                    for q in range(4)
                ]
                for t, tile in enumerate(block_transpose(parts)):
                    send3[u, 4 * cc + t, 16 * pair : 16 * pair + 16, :] = tile.astype(jnp.bfloat16)

        @pl.loop(1, COLS)
        def _(e):
            copy3(u, e).start()

        recv3[u, col] = send3[u, col]

        @pl.loop(1, COLS)
        def _(e):
            copy3(u, e).wait_recv()

        for half in range(2):
            for pair in range(4):
                first = recv3[u, 4 * pair + half].astype(jnp.float32)
                second = recv3[u, 4 * pair + 2 + half].astype(jnp.float32)
                for k in range(8):
                    tile = jnp.concatenate([first[8 * k : 8 * k + 8], second[8 * k : 8 * k + 8]], axis=0)
                    send4[u, 8 * half + k, 16 * pair : 16 * pair + 16, :] = tile.astype(jnp.bfloat16)

        @pl.loop(1, ROWS)
        def _(d):
            copy4(u, d).start()

        recv4[u, row] = send4[u, row]

        @pl.loop(1, ROWS)
        def _(d):
            copy4(u, d).wait_recv()

        total = jnp.zeros((SUB, 128), jnp.float32)
        for k in range(ROWS):
            total += jnp.sum(recv4[u, k].astype(jnp.float32).reshape(8, SUB, 128), axis=0)
        middle = total * (1.0 / CH)
        total = jnp.zeros((SUB, 128), jnp.float32)
        for k in range(ROWS):
            centred = recv4[u, k].astype(jnp.float32).reshape(8, SUB, 128) - middle
            total += jnp.sum(centred * centred, axis=0)
        scale = lax.rsqrt(total * (1.0 / CH) + 1e-05)
        for k in range(ROWS):
            centred = recv4[u, k].astype(jnp.float32).reshape(8, SUB, 128) - middle
            hidden[64 * k : 64 * k + 64, :] = (centred * scale).reshape(64, 128)
        for s in range(SUB):
            hidden_t[:, s * 128 : (s + 1) * 128] = hidden[pl.ds(s, CH, stride=SUB), :].astype(jnp.bfloat16)
        for j in range(4):
            cols = slice(256 * j, 256 * (j + 1))
            update = jnp.dot(final_t[u], hidden_t[:, cols], preferred_element_type=jnp.float32)
            result = pair_t[:, cols] + gate[:, cols] * update
            pair_t[:, cols] = result.astype(jnp.bfloat16).astype(jnp.float32)

    for s in range(SUB):
        block = pair_t[:, s * 128 : (s + 1) * 128].T.astype(jnp.bfloat16)
        for q in range(4):
            out_ref[8 * q + s] = block[32 * q : 32 * q + 32]

    for u in range(2):

        @pl.loop(1, 16)
        def _(d):
            copy1(u, d).wait_send()
            copy3(u, d).wait_send()
            copy4(u, d).wait_send()

            @pl.loop(0, CHUNKS)
            def _(g):
                copy2(u, g, d).wait_send()


def shards(pair_act, residue_mask, *weights):
    bf16, f32 = jnp.bfloat16, jnp.float32
    dma = pltpu.SemaphoreType.DMA
    vmem = pl.BlockSpec(memory_space=pltpu.VMEM)
    return pl.pallas_call(
        kernel,
        out_shape=jax.ShapeDtypeStruct(pair_act.shape, pair_act.dtype),
        in_specs=[pl.BlockSpec(memory_space=pltpu.SMEM)] + [vmem] * 5,
        out_specs=vmem,
        scratch_shapes=[
            pltpu.VMEM((CH, 1024), f32),
            pltpu.VMEM((2, 5 * CH, CH), bf16),
            pltpu.VMEM((2, CH, CH), bf16),
            pltpu.VMEM((SUB, 128), f32),
            pltpu.VMEM((CH, 1024), bf16),
            pltpu.VMEM((5 * CH, 1024), f32),
            pltpu.VMEM((CH, 1024), f32),
            pltpu.VMEM((128, 128), f32),
            pltpu.VMEM((2, ROWS, 8, 16, 128), bf16),
            pltpu.VMEM((2, ROWS, 8, 16, 128), bf16),
            pltpu.VMEM((2, COLS, ROWS, 16, 128), bf16),
            pltpu.VMEM((256, 512), bf16),
            pltpu.VMEM((512, 256), bf16),
            pltpu.VMEM((512, 512), bf16),
            pltpu.VMEM((256, 512), f32),
            pltpu.VMEM((2, COLS, 64, 128), bf16),
            pltpu.VMEM((2, COLS, 64, 128), bf16),
            pltpu.VMEM((2, ROWS, 64, 128), bf16),
            pltpu.VMEM((2, ROWS, 64, 128), bf16),
            pltpu.VMEM((1024, 128), f32),
            pltpu.VMEM((CH, 1024), bf16),
            dma((2, ROWS)), dma((2, ROWS)),
            dma((2, CHUNKS, COLS)), dma((2, CHUNKS, COLS)),
            dma((2, COLS)), dma((2, COLS)),
            dma((2, ROWS)), dma((2, ROWS)),
        ],
        compiler_params=pltpu.CompilerParams(
            collective_id=0, has_side_effects=True, vmem_limit_bytes=48 * 1024 * 1024
        ),
    )(residue_mask, pair_act, *weights)


def solution(mesh):
    return jax.shard_map(
        shards,
        mesh=mesh,
        in_specs=(P("row", "col", None), P(), P(), P(), P(), P()),
        out_specs=P("row", "col", None),
        check_vma=False,
    )
```

```python
import jax
import jax.numpy as jnp
from jax import lax
from jax.experimental import pallas as pl
from jax.experimental.pallas import tpu as pltpu
from jax.sharding import PartitionSpec as P

ROWS = 16
COLS = 16
CH = 128
BLK = 32
SUB = 8
CHUNKS = 4
PER = ROWS // CHUNKS
STEPS = (4, 3, -3, 2, -2, 1, -1, 0)
ZERO = STEPS.index(0)
SELF = 2 * ZERO
MESH = pl.DeviceIdType.MESH


def block_transpose(parts):
    lane = lax.broadcasted_iota(jnp.int32, parts[0].shape, 1)
    low = lane < 64
    even = (lane // 32) % 2 == 0
    t0, t1, t2, t3 = parts
    u0 = jnp.where(low, t0, pltpu.roll(t2, 64, 1))
    u2 = jnp.where(low, pltpu.roll(t0, 64, 1), t2)
    u1 = jnp.where(low, t1, pltpu.roll(t3, 64, 1))
    u3 = jnp.where(low, pltpu.roll(t1, 64, 1), t3)
    return (
        jnp.where(even, u0, pltpu.roll(u1, 32, 1)),
        jnp.where(even, pltpu.roll(u0, 96, 1), u1),
        jnp.where(even, u2, pltpu.roll(u3, 32, 1)),
        jnp.where(even, pltpu.roll(u2, 96, 1), u3),
    )


def kernel(
    mask_hbm, pair_hbm, w_out, f_out, w_in, f_in, out_ref,
    mask_ref, pair_ref, w_ref, f_ref,
    pair_t, weights_t, final_t, half_mask, normed, mixed, gate, stage,
    send1, recv1, left_o, left_i, right, summed, send3, recv3,
    hidden, hidden_t,
    s0, s1, r1, sf, rf, s3, r3, sg, rg,
):
    loads = [
        pltpu.make_async_copy(src, dst, s0.at[i])
        for i, (src, dst) in enumerate(
            (
                (pair_hbm, pair_ref), (w_out, w_ref.at[0]), (mask_hbm, mask_ref),
                (w_in, w_ref.at[1]), (f_out, f_ref.at[0]), (f_in, f_ref.at[1]),
            )
        )
    ]
    for load in loads:
        load.start()

    row, col = lax.axis_index("row"), lax.axis_index("col")
    y_lo, z = row // 8, row % 8
    x, y_hi, core = col // 4, (col // 2) % 2, col % 2
    chip = col // 2
    z_to = [(z + b + 8) % 8 for b in STEPS]
    z_from = [(z + 8 - b) % 8 for b in STEPS]
    y_at = [y_lo, 1 - y_lo]
    x_at = [(x + e) % 4 for e in range(4)]
    y_hi_at = [y_hi, 1 - y_hi]
    row_to = [y_at[d % 2] * 8 + z_to[d // 2] for d in range(ROWS)]
    row_back = [core * 8 + z_to[b] for b in range(8)]
    row_from = [y_at[d % 2] * 8 + z_from[d // 2] for d in range(ROWS)]
    chip_to = [x_at[e // 2] * 2 + y_hi_at[e % 2] for e in range(8)]
    col_to = [chip_to[e] * 2 + core for e in range(8)]
    sibling = {"col": chip * 2 + 1 - core}
    entry = y_lo == core

    barrier = pltpu.get_barrier_semaphore()
    for d in range(ROWS):
        for e in range(8):
            if (d, e) != (SELF, 0):
                pl.semaphore_signal(
                    barrier, inc=1, device_id={"row": row_to[d], "col": col_to[e]}, device_id_type=MESH
                )
    pl.semaphore_signal(barrier, inc=1, device_id=sibling, device_id_type=MESH)

    def remote(src, dst, ssem, rsem, to):
        return pltpu.make_async_remote_copy(
            src_ref=src, dst_ref=dst, send_sem=ssem, recv_sem=rsem,
            device_id=to, device_id_type=MESH,
        )

    def copy1(u, d, e):
        src = send1.at[u, d, chip_to[e]]
        dst = recv1.at[u, core, d // PER, d % PER, chip]
        if (d, e) == (SELF, 0):
            return pltpu.make_async_copy(src, dst, r1.at[u, d // PER])
        return remote(
            src, dst, s1.at[u, d], r1.at[u, d // PER], {"row": row_to[d], "col": col_to[e]}
        )

    def wait1(u, g):
        block = recv1.at[u, core, g]
        remote(block, block, s1.at[u, 0], r1.at[u, g], sibling).wait_recv()

    def forward1(u, g):
        block = recv1.at[u, core, g]
        return remote(block, block, sf.at[u, g], rf.at[u, g], sibling)

    def copy3(u, b, e):
        return remote(
            send3.at[u, b, chip_to[e]], recv3.at[u, row, chip], s3.at[u, b, int((b, e) == (ZERO, 0))],
            r3.at[u, b // 2], {"row": row_back[b], "col": col_to[e]},
        )

    def wait3(u, k):
        block = recv3.at[u, pl.ds(4 * k, 4)]
        remote(block, block, s3.at[u, 0, 0], r3.at[u, k], sibling).wait_recv()

    def forward3(u, d):
        block = recv3.at[u, row_from[d]]
        return remote(block, block, sg.at[u, d], rg.at[u, d], sibling)

    def turn_weights(u):
        weights_t[u] = w_ref[u].astype(jnp.float32).T.astype(jnp.bfloat16)

    loads[0].wait()
    for s in range(SUB):
        block = jnp.concatenate([pair_ref[8 * q + s] for q in range(4)], axis=0)
        pair_t[:, s * 128 : (s + 1) * 128] = block.astype(jnp.float32).T
    loads[1].wait()
    turn_weights(0)

    loads[2].wait()
    lane = lax.broadcasted_iota(jnp.int32, (SUB, 128), 1)
    sub = lax.broadcasted_iota(jnp.int32, (SUB, 128), 0)
    by_row = jnp.zeros((SUB, 128), jnp.float32)
    by_col = jnp.zeros((SUB, 128), jnp.float32)
    for k in range(BLK):
        by_col = jnp.where(lane % 32 == k, mask_ref[col * BLK + k].astype(jnp.float32), by_col)
        by_row = jnp.where(
            (lane // 32) * 8 + sub == k, mask_ref[row * BLK + k].astype(jnp.float32), by_row
        )
    half_mask[...] = 0.5 * by_row * by_col

    def project(u):
        for j in range(4):
            cols = slice(256 * j, 256 * (j + 1))
            values = pair_t[:, cols]
            middle = jnp.mean(values, axis=0, keepdims=True)
            centred = values - middle
            spread = jnp.mean(centred * centred, axis=0, keepdims=True)
            normed[:, cols] = (centred * lax.rsqrt(spread + 1e-05)).astype(jnp.bfloat16)
            mixed[:, cols] = jnp.dot(
                weights_t[u], normed[:, cols], preferred_element_type=jnp.float32
            )

    def sides(u, d):
        at = row_to[d] * 8
        held = stage.at[d % 2]

        def part(k):
            return mixed[pl.ds(pl.multiple_of(at + k * CH, 8), 8), :]

        for side in range(2):
            value, gates = part(2 * side), part(2 * side + 1)
            for s in range(SUB):
                cols = slice(s * 128, (s + 1) * 128)
                held[pl.ds(side * 8 + s, 8, stride=16), :] = (
                    (jnp.tanh(0.5 * gates[:, cols]) + 1.0) * value[:, cols] * half_mask[s : s + 1, :]
                )
        return held[...].astype(jnp.bfloat16).reshape(8, 16, 128)

    def tile_at(u, g, cc, t, i):
        return recv1[u, t % 2, g, i, 2 * cc + t // 2].astype(jnp.float32)

    def assemble_right(u, g):
        for cc in range(4):
            turned = block_transpose(
                [jnp.concatenate([tile_at(u, g, cc, t, i)[8:] for i in range(PER)], axis=0) for t in range(4)]
            )
            for i in range(PER):
                rows = jnp.concatenate([v[8 * i : 8 * i + 8] for v in turned], axis=0)
                at = pl.multiple_of(row_from[g * PER + i] * BLK, BLK)
                right[pl.ds(at, BLK), cc * 128 : (cc + 1) * 128] = rows.astype(jnp.bfloat16)

    def assemble_left_o(u, g):
        a = (core + y_lo) % 2
        for cc in range(4):
            turned = block_transpose(
                [
                    jnp.concatenate([tile_at(u, g, cc, t, 2 * i + a)[:8] for i in range(PER // 2)], axis=0)
                    for t in range(4)
                ]
            )
            for i in range(PER // 2):
                rows = jnp.concatenate([v[8 * i : 8 * i + 8] for v in turned], axis=0)
                at = pl.multiple_of(z_from[g * PER // 2 + i] * BLK, BLK)
                left_o[pl.ds(at, BLK), cc * 128 : (cc + 1) * 128] = rows.astype(jnp.bfloat16)

    def assemble_left_i(u, g):
        for cc in range(2):
            turned = block_transpose(
                [
                    jnp.concatenate([tile_at(u, g, 2 * core + cc, t, i)[:8] for i in range(PER)], axis=0)
                    for t in range(4)
                ]
            )
            for i in range(PER):
                rows = jnp.concatenate([v[8 * i : 8 * i + 8] for v in turned], axis=0)
                at = pl.multiple_of(row_from[g * PER + i] * BLK, BLK)
                left_i[pl.ds(at, BLK), cc * 128 : (cc + 1) * 128] = rows.astype(jnp.bfloat16)

    def assemble(u, g):
        forward1(u, g).wait_recv()
        assemble_right(u, g)
        if u == 0:
            assemble_left_o(u, g)
        else:
            assemble_left_i(u, g)

    for u in range(2):
        project(u)
        if u == 0:
            pl.semaphore_wait(barrier, 128)

        for d in range(ROWS):
            send1[u, d] = sides(u, d)
            for e in range(8):
                copy1(u, d, e).start()

        gate[...] = 0.5 * jnp.tanh(0.5 * mixed[4 * CH :, :]) + 0.5
        if u == 0:
            for load in loads[3:]:
                load.wait()
            turn_weights(1)
            for k in range(2):
                final_t[k] = f_ref[k].astype(jnp.float32).T.astype(jnp.bfloat16)

        for g in range(CHUNKS):
            wait1(u, g)
            forward1(u, g).start()
            if g >= 1:
                assemble(u, g - 1)
        assemble(u, CHUNKS - 1)

        if u == 0:
            summed[...] = lax.dot_general(
                left_o[...], right[...], (((1,), (1,)), ((), ())), preferred_element_type=jnp.float32
            )
        else:
            summed[...] = lax.dot_general(
                left_i[...], right[...], (((0,), (0,)), ((), ())), preferred_element_type=jnp.float32
            )

        for b in range(8):
            for cc in range(4):
                turned = block_transpose(
                    [
                        summed[
                            pl.ds(pl.multiple_of(z_to[b] * BLK + 8 * q, 8), 8),
                            cc * 128 : (cc + 1) * 128,
                        ]
                        for q in range(4)
                    ]
                )
                for k in range(2):
                    tile = jnp.concatenate(turned[2 * k : 2 * k + 2], axis=0)
                    send3[u, b, 2 * cc + k] = tile.astype(jnp.bfloat16)
            for e in range(8):
                if (b, e) != (ZERO, 0):
                    copy3(u, b, e).start()
                else:

                    @pl.when(entry)
                    def _():
                        own = pltpu.make_async_copy(
                            send3.at[u, b, chip], recv3.at[u, row, chip], r3.at[u, b // 2]
                        )
                        own.start()

                    @pl.when(jnp.logical_not(entry))
                    def _():
                        copy3(u, b, e).start()

        @pl.when(entry)
        def _():
            for k in range(4):
                wait3(u, k)
                for d in range(4 * k, 4 * k + 4):
                    forward3(u, d).start()

        @pl.when(jnp.logical_not(entry))
        def _():
            for d in range(ROWS):
                forward3(u, d).wait_recv()

        def sums(k):
            both = recv3[u, k].astype(jnp.float32)
            return jnp.where(core == 0, both[:, :8], both[:, 8:])

        total = jnp.zeros((SUB, 128), jnp.float32)
        for k in range(ROWS):
            total += jnp.sum(sums(k), axis=0)
        middle = total * (1.0 / CH)
        total = jnp.zeros((SUB, 128), jnp.float32)
        for k in range(ROWS):
            centred = sums(k) - middle
            total += jnp.sum(centred * centred, axis=0)
        scale = lax.rsqrt(total * (1.0 / CH) + 1e-05)
        for k in range(ROWS):
            centred = sums(k) - middle
            hidden[64 * k : 64 * k + 64, :] = (centred * scale).reshape(64, 128)
        for s in range(SUB):
            hidden_t[:, s * 128 : (s + 1) * 128] = hidden[pl.ds(s, CH, stride=SUB), :].astype(jnp.bfloat16)
        for j in range(4):
            cols = slice(256 * j, 256 * (j + 1))
            update = jnp.dot(final_t[u], hidden_t[:, cols], preferred_element_type=jnp.float32)
            result = pair_t[:, cols] + gate[:, cols] * update
            pair_t[:, cols] = result.astype(jnp.bfloat16).astype(jnp.float32)

    for s in range(SUB):
        block = pair_t[:, s * 128 : (s + 1) * 128].T.astype(jnp.bfloat16)
        for q in range(4):
            out_ref[8 * q + s] = block[32 * q : 32 * q + 32]

    for u in range(2):
        for d in range(ROWS):
            count = 7 if d == SELF else 8
            remote(
                send1.at[u, d, pl.ds(0, count)], send1.at[u, d, pl.ds(0, count)],
                s1.at[u, d], r1.at[u, 0], sibling,
            ).wait_send()
        for g in range(CHUNKS):
            forward1(u, g).wait_send()
        for b in range(8):
            count = 7 if b == ZERO else 8
            remote(
                send3.at[u, b, pl.ds(0, count)], send3.at[u, b, pl.ds(0, count)],
                s3.at[u, b, 0], r3.at[u, 0], sibling,
            ).wait_send()

        @pl.when(entry)
        def _():
            for d in range(ROWS):
                forward3(u, d).wait_send()

        @pl.when(jnp.logical_not(entry))
        def _():
            copy3(u, ZERO, 0).wait_send()


def shards(pair_act, residue_mask, *weights):
    bf16, f32 = jnp.bfloat16, jnp.float32
    dma = pltpu.SemaphoreType.DMA
    vmem = pl.BlockSpec(memory_space=pltpu.VMEM)
    return pl.pallas_call(
        kernel,
        out_shape=jax.ShapeDtypeStruct(pair_act.shape, pair_act.dtype),
        in_specs=[pl.BlockSpec(memory_space=pl.ANY)] * 6,
        out_specs=vmem,
        scratch_shapes=[
            pltpu.SMEM(residue_mask.shape, jnp.int32),
            pltpu.VMEM(pair_act.shape, bf16),
            pltpu.VMEM((2, CH, 5 * CH), bf16),
            pltpu.VMEM((2, CH, CH), bf16),
            pltpu.VMEM((CH, 1024), f32),
            pltpu.VMEM((2, 5 * CH, CH), bf16),
            pltpu.VMEM((2, CH, CH), bf16),
            pltpu.VMEM((SUB, 128), f32),
            pltpu.VMEM((CH, 1024), bf16),
            pltpu.VMEM((5 * CH, 1024), f32),
            pltpu.VMEM((CH, 1024), f32),
            pltpu.VMEM((2, 128, 128), f32),
            pltpu.VMEM((2, ROWS, 8, 16, 128), bf16),
            pltpu.VMEM((2, 2, CHUNKS, PER, 8, 16, 128), bf16),
            pltpu.VMEM((256, 512), bf16),
            pltpu.VMEM((512, 256), bf16),
            pltpu.VMEM((512, 512), bf16),
            pltpu.VMEM((256, 512), f32),
            pltpu.VMEM((2, 8, 8, 16, 128), bf16),
            pltpu.VMEM((2, ROWS, 8, 16, 128), bf16),
            pltpu.VMEM((1024, 128), f32),
            pltpu.VMEM((CH, 1024), bf16),
            dma((6,)),
            dma((2, ROWS)), dma((2, CHUNKS)),
            dma((2, CHUNKS)), dma((2, CHUNKS)),
            dma((2, 8, 2)), dma((2, 4)),
            dma((2, ROWS)), dma((2, ROWS)),
        ],
        compiler_params=pltpu.CompilerParams(
            collective_id=0, has_side_effects=True, vmem_limit_bytes=60 * 1024 * 1024
        ),
    )(residue_mask, pair_act, *weights)


def solution(mesh):
    return jax.shard_map(
        shards,
        mesh=mesh,
        in_specs=(P("row", "col", None), P(), P(), P(), P(), P()),
        out_specs=P("row", "col", None),
        check_vma=False,
    )
```

```python
import jax
import jax.numpy as jnp
from jax import lax
from jax.experimental import pallas as pl
from jax.experimental.pallas import tpu as pltpu
from jax.sharding import PartitionSpec as P

ROWS = 16
COLS = 16
CH = 128
BLK = 32
SUB = 8
CHUNKS = 4
PER = ROWS // CHUNKS
STEPS = (4, 3, -3, 2, -2, 1, -1, 0)
SELF = 2 * STEPS.index(0)
EVEN, ODD = (4, 2, -2, 0), (3, -3, 1, -1)
LAST = 2 * EVEN.index(0)
MESH = pl.DeviceIdType.MESH


def block_transpose(parts):
    lane = lax.broadcasted_iota(jnp.int32, parts[0].shape, 1)
    low = lane < 64
    even = (lane // 32) % 2 == 0
    t0, t1, t2, t3 = parts
    u0 = jnp.where(low, t0, pltpu.roll(t2, 64, 1))
    u2 = jnp.where(low, pltpu.roll(t0, 64, 1), t2)
    u1 = jnp.where(low, t1, pltpu.roll(t3, 64, 1))
    u3 = jnp.where(low, pltpu.roll(t1, 64, 1), t3)
    return (
        jnp.where(even, u0, pltpu.roll(u1, 32, 1)),
        jnp.where(even, pltpu.roll(u0, 96, 1), u1),
        jnp.where(even, u2, pltpu.roll(u3, 32, 1)),
        jnp.where(even, pltpu.roll(u2, 96, 1), u3),
    )


def kernel(
    mask_hbm, pair_hbm, w_out, f_out, w_in, f_in, out_ref,
    mask_ref, pair_ref, w_ref, f_ref,
    pair_t, weights_t, final_t, half_mask, normed, mixed, gate, stage,
    send1, recv1, left, right_o, right_i, summed, send3, recv3,
    hidden, hidden_t,
    s0, s1, r1, sf, rf, s3, r3, sx,
):
    loads = [
        pltpu.make_async_copy(src, dst, s0.at[i])
        for i, (src, dst) in enumerate(
            (
                (pair_hbm, pair_ref), (w_out, w_ref.at[0]), (mask_hbm, mask_ref),
                (w_in, w_ref.at[1]), (f_out, f_ref.at[0]), (f_in, f_ref.at[1]),
            )
        )
    ]
    for load in loads:
        load.start()

    row, col = lax.axis_index("row"), lax.axis_index("col")
    y_lo, z = row // 8, row % 8
    x, y_hi, core = col // 4, (col // 2) % 2, col % 2
    chip = col // 2
    z_to = [(z + b + 8) % 8 for b in STEPS]
    z_from = [(z + 8 - b) % 8 for b in STEPS]
    y_at = [y_lo, 1 - y_lo]
    core_at = [core, 1 - core]
    x_at = [(x + e) % 4 for e in range(4)]
    y_hi_at = [y_hi, 1 - y_hi]
    row_to = [y_at[d % 2] * 8 + z_to[d // 2] for d in range(ROWS)]
    odd = [(z + core) % 2, (z + core + 1) % 2]
    z_part = [
        [(z + 8 + EVEN[j] + odd[part] * (ODD[j] - EVEN[j])) % 8 for j in range(4)] for part in range(2)
    ]
    row_part = [[y_at[k % 2] * 8 + z_part[part][k // 2] for k in range(8)] for part in range(2)]
    row_from = [y_at[d % 2] * 8 + z_from[d // 2] for d in range(ROWS)]
    chip_to = [x_at[e // 2] * 2 + y_hi_at[e % 2] for e in range(8)]
    col_to = [chip_to[e] * 2 + core for e in range(8)]
    sibling = {"col": chip * 2 + 1 - core}

    barrier = pltpu.get_barrier_semaphore()
    for d in range(ROWS):
        for e in range(8):
            if (d, e) != (SELF, 0):
                pl.semaphore_signal(
                    barrier, inc=1, device_id={"row": row_to[d], "col": col_to[e]}, device_id_type=MESH
                )
    pl.semaphore_signal(barrier, inc=1, device_id=sibling, device_id_type=MESH)

    def remote(src, dst, ssem, rsem, to):
        return pltpu.make_async_remote_copy(
            src_ref=src, dst_ref=dst, send_sem=ssem, recv_sem=rsem,
            device_id=to, device_id_type=MESH,
        )

    def copy1(u, d, e):
        src = send1.at[u, d, chip_to[e]]
        dst = recv1.at[u, core, d // PER, d % PER, chip]
        if (d, e) == (SELF, 0):
            return pltpu.make_async_copy(src, dst, r1.at[u, d // PER])
        return remote(
            src, dst, s1.at[u, d], r1.at[u, d // PER], {"row": row_to[d], "col": col_to[e]}
        )

    def wait1(u, g):
        block = recv1.at[u, core, g]
        remote(block, block, sx, r1.at[u, g], sibling).wait_recv()

    def forward1(u, g):
        block = recv1.at[u, core, g] if u == 0 else recv1.at[u, core, g, :, :, 0]
        return remote(block, block, sf.at[u, g], rf.at[u, g], sibling)

    def send_sums(u, slot, to_row, e, own):
        src, dst = send3.at[u, slot, chip_to[e]], recv3.at[u, row, chip]
        to = {"row": to_row, "col": col_to[e]}

        def here():
            pltpu.make_async_copy(src, dst, r3.at[u]).start()

        if own is None:
            remote(src, dst, s3.at[u, slot], r3.at[u], to).start()
        elif own is True:
            here()
        else:
            pl.when(own)(here)

            @pl.when(jnp.logical_not(own))
            def _():
                remote(src, dst, sx, r3.at[u], to).start()

    def wait_sums(u):
        block = recv3.at[u]
        remote(block, block, sx, r3.at[u], sibling).wait_recv()

    def turn_weights(u):
        weights_t[u] = w_ref[u].astype(jnp.float32).T.astype(jnp.bfloat16)

    loads[0].wait()
    for s in range(SUB):
        block = jnp.concatenate([pair_ref[8 * q + s] for q in range(4)], axis=0)
        pair_t[:, s * 128 : (s + 1) * 128] = block.astype(jnp.float32).T
    loads[1].wait()
    turn_weights(0)

    loads[2].wait()
    lane = lax.broadcasted_iota(jnp.int32, (SUB, 128), 1)
    sub = lax.broadcasted_iota(jnp.int32, (SUB, 128), 0)
    by_row = jnp.zeros((SUB, 128), jnp.float32)
    by_col = jnp.zeros((SUB, 128), jnp.float32)
    for k in range(BLK):
        by_col = jnp.where(lane % 32 == k, mask_ref[col * BLK + k].astype(jnp.float32), by_col)
        by_row = jnp.where(
            (lane // 32) * 8 + sub == k, mask_ref[row * BLK + k].astype(jnp.float32), by_row
        )
    half_mask[...] = 0.5 * by_row * by_col

    def project(u):
        for j in range(4):
            cols = slice(256 * j, 256 * (j + 1))
            values = pair_t[:, cols]
            middle = jnp.mean(values, axis=0, keepdims=True)
            centred = values - middle
            spread = jnp.mean(centred * centred, axis=0, keepdims=True)
            normed[:, cols] = (centred * lax.rsqrt(spread + 1e-05)).astype(jnp.bfloat16)
            mixed[:, cols] = jnp.dot(
                weights_t[u], normed[:, cols], preferred_element_type=jnp.float32
            )

    def sides(u, d):
        at = row_to[d] * 8
        held = stage.at[d % 2]

        def part(k):
            return mixed[pl.ds(pl.multiple_of(at + k * CH, 8), 8), :]

        for side in range(2):
            value, gates = part(2 * side), part(2 * side + 1)
            for s in range(SUB):
                cols = slice(s * 128, (s + 1) * 128)
                held[pl.ds(side * 8 + s, 8, stride=16), :] = (
                    (jnp.tanh(0.5 * gates[:, cols]) + 1.0) * value[:, cols] * half_mask[s : s + 1, :]
                )
        return held[...].astype(jnp.bfloat16).reshape(8, 2, SUB, 128)

    def turned_tiles(u, k, g, slots, v, side):
        turned = block_transpose(
            [
                jnp.concatenate(
                    [recv1[u, k, g, i, 4 * v + t, side].astype(jnp.float32) for i in slots], axis=0
                )
                for t in range(4)
            ]
        )
        return [
            jnp.concatenate([w[8 * i : 8 * i + 8] for w in turned], axis=0).astype(jnp.bfloat16)
            for i in range(len(slots))
        ]

    def band(r):
        return pl.ds(pl.multiple_of(r * BLK, BLK), BLK)

    def assemble(u, g, part):
        k = core_at[part]
        for v in range(2):
            lanes = slice(256 * part + 128 * v, 256 * part + 128 * v + 128)
            for i, rows in enumerate(turned_tiles(u, k, g, range(PER), v, 0)):
                left[band(row_from[g * PER + i]), lanes] = rows
            if u == 0:
                step = (z + core + g) % 2
                z_src = z_from[2 * g] + step * (z_from[2 * g + 1] - z_from[2 * g])
                slots = [2 * step + a for a in range(2)]
                for a, rows in enumerate(turned_tiles(u, k, g, slots, v, 1)):
                    right_o[band(y_at[a] * 4 + z_src // 2), lanes] = rows
            elif part == 0:
                for i, rows in enumerate(turned_tiles(u, k, g, range(PER), v, 1)):
                    right_i[band(row_from[g * PER + i]), lanes] = rows

    def back(u, slot, to_row, at, own):
        for v in range(2):
            turned = block_transpose(
                [
                    summed[pl.ds(pl.multiple_of(at + 8 * q, 8), 8), 128 * v : 128 * v + 128]
                    for q in range(4)
                ]
            )
            for t, tile in enumerate(turned):
                send3[u, slot, 4 * v + t] = tile.astype(jnp.bfloat16)
        for e in range(8):
            send_sums(u, slot, to_row, e, own if e == 0 else None)

    for u in range(2):
        project(u)
        if u == 0:
            pl.semaphore_wait(barrier, 128)

        for d in range(ROWS):
            send1[u, d] = sides(u, d)
            for e in range(8):
                copy1(u, d, e).start()

        gate[...] = 0.5 * jnp.tanh(0.5 * mixed[4 * CH :, :]) + 0.5
        if u == 0:
            for load in loads[3:]:
                load.wait()
            turn_weights(1)
            for k in range(2):
                final_t[k] = f_ref[k].astype(jnp.float32).T.astype(jnp.bfloat16)

        for g in range(CHUNKS):
            wait1(u, g)
            forward1(u, g).start()
            assemble(u, g, 0)

        if u == 0:
            for part in range(2):
                if part == 1:
                    for g in range(CHUNKS):
                        forward1(u, g).wait_recv()
                        assemble(u, g, 1)
                lanes = slice(256 * part, 256 * part + 256)
                term = lax.dot_general(
                    left[:, lanes], right_o[:, lanes], (((1,), (1,)), ((), ())),
                    preferred_element_type=jnp.float32,
                )
                summed[...] = term if part == 0 else summed[...] + term
            for d in range(ROWS):
                back(u, d, row_to[d], row_to[d] * BLK, True if d == SELF else None)
        else:
            for part in range(2):
                if part == 1:
                    for g in range(CHUNKS):
                        forward1(u, g).wait_recv()
                        assemble(u, g, 1)
                lanes = slice(256 * part, 256 * part + 256)
                summed[lanes, :] = lax.dot_general(
                    left[:, lanes], right_i[...], (((0,), (0,)), ((), ())),
                    preferred_element_type=jnp.float32,
                )
                for k in range(8):
                    at = 256 * part + (y_at[k % 2] * 4 + z_part[part][k // 2] // 2) * BLK
                    own = odd[part] == 0 if k == LAST else None
                    back(u, 8 * part + k, row_part[part][k], at, own)

        wait_sums(u)

        def sums(k):
            return recv3[u, k].astype(jnp.float32)

        total = jnp.zeros((SUB, 128), jnp.float32)
        for k in range(ROWS):
            total += jnp.sum(sums(k), axis=0)
        middle = total * (1.0 / CH)
        total = jnp.zeros((SUB, 128), jnp.float32)
        for k in range(ROWS):
            centred = sums(k) - middle
            total += jnp.sum(centred * centred, axis=0)
        scale = lax.rsqrt(total * (1.0 / CH) + 1e-05)
        for k in range(ROWS):
            centred = sums(k) - middle
            hidden[64 * k : 64 * k + 64, :] = (centred * scale).reshape(64, 128)
        for s in range(SUB):
            hidden_t[:, s * 128 : (s + 1) * 128] = hidden[pl.ds(s, CH, stride=SUB), :].astype(jnp.bfloat16)
        for j in range(4):
            cols = slice(256 * j, 256 * (j + 1))
            update = jnp.dot(final_t[u], hidden_t[:, cols], preferred_element_type=jnp.float32)
            result = pair_t[:, cols] + gate[:, cols] * update
            pair_t[:, cols] = result.astype(jnp.bfloat16).astype(jnp.float32)

    for s in range(SUB):
        block = pair_t[:, s * 128 : (s + 1) * 128].T.astype(jnp.bfloat16)
        for q in range(4):
            out_ref[8 * q + s] = block[32 * q : 32 * q + 32]

    for u in range(2):
        for d in range(ROWS):
            count = 7 if d == SELF else 8
            remote(
                send1.at[u, d, pl.ds(0, count)], send1.at[u, d, pl.ds(0, count)],
                s1.at[u, d], r1.at[u, 0], sibling,
            ).wait_send()
        for g in range(CHUNKS):
            forward1(u, g).wait_send()
        for slot in range(ROWS):
            count = 7 if slot in ((SELF,), (LAST, 8 + LAST))[u] else 8
            block = send3.at[u, slot, pl.ds(0, count)]
            remote(block, block, s3.at[u, slot], r3.at[u], sibling).wait_send()
    remote(send3.at[1, 0, 0], send3.at[1, 0, 0], sx, r3.at[1], sibling).wait_send()


def shards(pair_act, residue_mask, *weights):
    bf16, f32 = jnp.bfloat16, jnp.float32
    dma = pltpu.SemaphoreType.DMA
    vmem = pl.BlockSpec(memory_space=pltpu.VMEM)
    return pl.pallas_call(
        kernel,
        out_shape=jax.ShapeDtypeStruct(pair_act.shape, pair_act.dtype),
        in_specs=[pl.BlockSpec(memory_space=pl.ANY)] * 6,
        out_specs=vmem,
        scratch_shapes=[
            pltpu.SMEM(residue_mask.shape, jnp.int32),
            pltpu.VMEM(pair_act.shape, bf16),
            pltpu.VMEM((2, CH, 5 * CH), bf16),
            pltpu.VMEM((2, CH, CH), bf16),
            pltpu.VMEM((CH, 1024), f32),
            pltpu.VMEM((2, 5 * CH, CH), bf16),
            pltpu.VMEM((2, CH, CH), bf16),
            pltpu.VMEM((SUB, 128), f32),
            pltpu.VMEM((CH, 1024), bf16),
            pltpu.VMEM((5 * CH, 1024), f32),
            pltpu.VMEM((CH, 1024), f32),
            pltpu.VMEM((2, 128, 128), f32),
            pltpu.VMEM((2, ROWS, 8, 2, SUB, 128), bf16),
            pltpu.VMEM((2, 2, CHUNKS, PER, 8, 2, SUB, 128), bf16),
            pltpu.VMEM((512, 512), bf16),
            pltpu.VMEM((256, 512), bf16),
            pltpu.VMEM((512, 256), bf16),
            pltpu.VMEM((512, 256), f32),
            pltpu.VMEM((2, ROWS, 8, SUB, 128), bf16),
            pltpu.VMEM((2, ROWS, 8, SUB, 128), bf16),
            pltpu.VMEM((1024, 128), f32),
            pltpu.VMEM((CH, 1024), bf16),
            dma((6,)),
            dma((2, ROWS)), dma((2, CHUNKS)),
            dma((2, CHUNKS)), dma((2, CHUNKS)),
            dma((2, ROWS)), dma((2,)), dma,
        ],
        compiler_params=pltpu.CompilerParams(
            collective_id=0, has_side_effects=True, vmem_limit_bytes=60 * 1024 * 1024
        ),
    )(residue_mask, pair_act, *weights)


def solution(mesh):
    return jax.shard_map(
        shards,
        mesh=mesh,
        in_specs=(P("row", "col", None), P(), P(), P(), P(), P()),
        out_specs=P("row", "col", None),
        check_vma=False,
    )
```

```python
import jax
import jax.numpy as jnp
from jax import lax
from jax.experimental import pallas as pl
from jax.experimental.pallas import tpu as pltpu
from jax.sharding import PartitionSpec as P

ROWS = 16
COLS = 16
CH = 128
BLK = 32
SUB = 8
CHUNKS = 4
PER = ROWS // CHUNKS
STEPS = (4, 3, -3, 2, -2, 1, -1, 0)
SELF = 2 * STEPS.index(0)
EVEN, ODD = (4, 2, -2, 0), (3, -3, 1, -1)
LAST = 2 * EVEN.index(0)
MESH = pl.DeviceIdType.MESH


def far_first(slots, steps=STEPS):
    def hops(to):
        d, e = to
        return abs(steps[d // 2]) + (0, 1, 2, 1)[e // 2] + ((0, 2), (1, 1))[d % 2][e % 2]

    return sorted(((d, e) for d in slots for e in range(8)), key=hops, reverse=True)


def block_transpose(parts):
    lane = lax.broadcasted_iota(jnp.int32, parts[0].shape, 1)
    low = lane < 64
    even = (lane // 32) % 2 == 0
    t0, t1, t2, t3 = parts
    u0 = jnp.where(low, t0, pltpu.roll(t2, 64, 1))
    u2 = jnp.where(low, pltpu.roll(t0, 64, 1), t2)
    u1 = jnp.where(low, t1, pltpu.roll(t3, 64, 1))
    u3 = jnp.where(low, pltpu.roll(t1, 64, 1), t3)
    return (
        jnp.where(even, u0, pltpu.roll(u1, 32, 1)),
        jnp.where(even, pltpu.roll(u0, 96, 1), u1),
        jnp.where(even, u2, pltpu.roll(u3, 32, 1)),
        jnp.where(even, pltpu.roll(u2, 96, 1), u3),
    )


def kernel(
    mask_hbm, pair_hbm, w_out, f_out, w_in, f_in, out_ref,
    mask_ref, pair_ref, w_ref, f_ref,
    pair_t, weights_t, final_t, half_mask, normed, mixed, gate, stage,
    send1, recv1, left, right_o, right_i, summed, send3, recv3,
    hidden, hidden_t,
    s0, s1, r1, sf, rf, s3, r3, sx,
):
    loads = [
        pltpu.make_async_copy(src, dst, s0.at[i])
        for i, (src, dst) in enumerate(
            (
                (pair_hbm, pair_ref), (w_out, w_ref.at[0]), (mask_hbm, mask_ref),
                (w_in, w_ref.at[1]), (f_out, f_ref.at[0]), (f_in, f_ref.at[1]),
            )
        )
    ]
    for load in loads:
        load.start()

    row, col = lax.axis_index("row"), lax.axis_index("col")
    y_lo, z = row // 8, row % 8
    x, y_hi, core = col // 4, (col // 2) % 2, col % 2
    chip = col // 2
    z_to = [(z + b + 8) % 8 for b in STEPS]
    z_from = [(z + 8 - b) % 8 for b in STEPS]
    y_at = [y_lo, 1 - y_lo]
    core_at = [core, 1 - core]
    x_at = [(x + e) % 4 for e in range(4)]
    y_hi_at = [y_hi, 1 - y_hi]
    row_to = [y_at[d % 2] * 8 + z_to[d // 2] for d in range(ROWS)]
    odd = [(z + core) % 2, (z + core + 1) % 2]
    z_part = [
        [(z + 8 + EVEN[j] + odd[part] * (ODD[j] - EVEN[j])) % 8 for j in range(4)] for part in range(2)
    ]
    row_part = [[y_at[k % 2] * 8 + z_part[part][k // 2] for k in range(8)] for part in range(2)]
    row_from = [y_at[d % 2] * 8 + z_from[d // 2] for d in range(ROWS)]
    chip_to = [x_at[e // 2] * 2 + y_hi_at[e % 2] for e in range(8)]
    col_to = [chip_to[e] * 2 + core for e in range(8)]
    sibling = {"col": chip * 2 + 1 - core}

    barrier = pltpu.get_barrier_semaphore()
    for d in range(ROWS):
        for e in range(8):
            if (d, e) != (SELF, 0):
                pl.semaphore_signal(
                    barrier, inc=1, device_id={"row": row_to[d], "col": col_to[e]}, device_id_type=MESH
                )
    pl.semaphore_signal(barrier, inc=1, device_id=sibling, device_id_type=MESH)

    def remote(src, dst, ssem, rsem, to):
        return pltpu.make_async_remote_copy(
            src_ref=src, dst_ref=dst, send_sem=ssem, recv_sem=rsem,
            device_id=to, device_id_type=MESH,
        )

    def copy1(u, d, e):
        src = send1.at[u, d, chip_to[e]]
        dst = recv1.at[u, core, d // PER, d % PER, chip]
        if (d, e) == (SELF, 0):
            return pltpu.make_async_copy(src, dst, r1.at[u, d // PER])
        return remote(
            src, dst, s1.at[u, d], r1.at[u, d // PER], {"row": row_to[d], "col": col_to[e]}
        )

    def wait1(u, g):
        block = recv1.at[u, core, g]
        remote(block, block, sx, r1.at[u, g], sibling).wait_recv()

    def forward1(u, g):
        block = recv1.at[u, core, g] if u == 0 else recv1.at[u, core, g, :, :, 0]
        return remote(block, block, sf.at[u, g], rf.at[u, g], sibling)

    def send_sums(u, slot, to_row, e, own):
        src, dst = send3.at[u, slot, chip_to[e]], recv3.at[u, row, chip]
        to = {"row": to_row, "col": col_to[e]}

        def here():
            pltpu.make_async_copy(src, dst, r3.at[u]).start()

        if own is None:
            remote(src, dst, s3.at[u, slot], r3.at[u], to).start()
        elif own is True:
            here()
        else:
            pl.when(own)(here)

            @pl.when(jnp.logical_not(own))
            def _():
                remote(src, dst, sx, r3.at[u], to).start()

    def wait_sums(u):
        block = recv3.at[u]
        remote(block, block, sx, r3.at[u], sibling).wait_recv()

    def turn_weights(u):
        weights_t[u] = w_ref[u].astype(jnp.float32).T.astype(jnp.bfloat16)

    loads[0].wait()
    for s in range(SUB):
        block = jnp.concatenate([pair_ref[8 * q + s] for q in range(4)], axis=0)
        pair_t[:, s * 128 : (s + 1) * 128] = block.astype(jnp.float32).T
    loads[1].wait()
    turn_weights(0)

    loads[2].wait()
    lane = lax.broadcasted_iota(jnp.int32, (SUB, 128), 1)
    sub = lax.broadcasted_iota(jnp.int32, (SUB, 128), 0)
    by_row = jnp.zeros((SUB, 128), jnp.float32)
    by_col = jnp.zeros((SUB, 128), jnp.float32)
    for k in range(BLK):
        by_col = jnp.where(lane % 32 == k, mask_ref[col * BLK + k].astype(jnp.float32), by_col)
        by_row = jnp.where(
            (lane // 32) * 8 + sub == k, mask_ref[row * BLK + k].astype(jnp.float32), by_row
        )
    half_mask[...] = 0.5 * by_row * by_col

    def project(u):
        for j in range(4):
            cols = slice(256 * j, 256 * (j + 1))
            values = pair_t[:, cols]
            middle = jnp.mean(values, axis=0, keepdims=True)
            centred = values - middle
            spread = jnp.mean(centred * centred, axis=0, keepdims=True)
            normed[:, cols] = (centred * lax.rsqrt(spread + 1e-05)).astype(jnp.bfloat16)
            mixed[:, cols] = jnp.dot(
                weights_t[u], normed[:, cols], preferred_element_type=jnp.float32
            )

    def sides(u, d):
        at = row_to[d] * 8
        held = stage.at[d % 2]

        def part(k):
            return mixed[pl.ds(pl.multiple_of(at + k * CH, 8), 8), :]

        for side in range(2):
            value, gates = part(2 * side), part(2 * side + 1)
            for s in range(SUB):
                cols = slice(s * 128, (s + 1) * 128)
                held[pl.ds(side * 8 + s, 8, stride=16), :] = (
                    (jnp.tanh(0.5 * gates[:, cols]) + 1.0) * value[:, cols] * half_mask[s : s + 1, :]
                )
        return held[...].astype(jnp.bfloat16).reshape(8, 2, SUB, 128)

    def turned_tiles(u, k, g, slots, v, side):
        turned = block_transpose(
            [
                jnp.concatenate(
                    [recv1[u, k, g, i, 4 * v + t, side] for i in slots], axis=0
                )
                for t in range(4)
            ]
        )
        return [
            jnp.concatenate([w[8 * i : 8 * i + 8] for w in turned], axis=0)
            for i in range(len(slots))
        ]

    def band(r):
        return pl.ds(pl.multiple_of(r * BLK, BLK), BLK)

    def assemble(u, g, part):
        k = core_at[part]
        for v in range(2):
            lanes = slice(256 * part + 128 * v, 256 * part + 128 * v + 128)
            for i, rows in enumerate(turned_tiles(u, k, g, range(PER), v, 0)):
                left[band(row_from[g * PER + i]), lanes] = rows
            if u == 0:
                step = (z + core + g) % 2
                z_src = z_from[2 * g] + step * (z_from[2 * g + 1] - z_from[2 * g])
                slots = [2 * step + a for a in range(2)]
                for a, rows in enumerate(turned_tiles(u, k, g, slots, v, 1)):
                    right_o[band(y_at[a] * 4 + z_src // 2), lanes] = rows
            elif part == 0:
                for i, rows in enumerate(turned_tiles(u, k, g, range(PER), v, 1)):
                    right_i[band(row_from[g * PER + i]), lanes] = rows

    def turn_sums(u, slots, at):
        for v in range(2):
            turned = block_transpose(
                [
                    jnp.concatenate(
                        [
                            summed[pl.ds(pl.multiple_of(a + 8 * q, 8), 8), 128 * v : 128 * v + 128]
                            for a in at
                        ],
                        axis=0,
                    )
                    for q in range(4)
                ]
            )
            for t, tiles in enumerate(turned):
                for i, slot in enumerate(slots):
                    send3[u, slot, 4 * v + t] = tiles[8 * i : 8 * i + 8].astype(jnp.bfloat16)

    for u in range(2):
        project(u)
        if u == 0:
            pl.semaphore_wait(barrier, 128)

        for g in range(CHUNKS):
            slots = range(g * PER, (g + 1) * PER)
            for d in slots:
                send1[u, d] = sides(u, d)
            for d, e in far_first(slots):
                copy1(u, d, e).start()

        gate[...] = 0.5 * jnp.tanh(0.5 * mixed[4 * CH :, :]) + 0.5
        if u == 0:
            for load in loads[3:]:
                load.wait()
            turn_weights(1)
            for k in range(2):
                final_t[k] = f_ref[k].astype(jnp.float32).T.astype(jnp.bfloat16)

        for g in range(CHUNKS):
            wait1(u, g)
            forward1(u, g).start()
            assemble(u, g, 0)

        if u == 0:
            for part in range(2):
                if part == 1:
                    for g in range(CHUNKS):
                        forward1(u, g).wait_recv()
                        assemble(u, g, 1)
                lanes = slice(256 * part, 256 * part + 256)
                term = lax.dot_general(
                    left[:, lanes], right_o[:, lanes], (((1,), (1,)), ((), ())),
                    preferred_element_type=jnp.float32,
                )
                summed[...] = term if part == 0 else summed[...] + term
            for g in range(4):
                slots = range(4 * g, 4 * g + 4)
                turn_sums(u, slots, [row_to[d] * BLK for d in slots])
            for d, e in far_first(range(ROWS)):
                send_sums(u, d, row_to[d], e, True if (d, e) == (SELF, 0) else None)
        else:
            for part in range(2):
                if part == 1:
                    for g in range(CHUNKS):
                        forward1(u, g).wait_recv()
                        assemble(u, g, 1)
                lanes = slice(256 * part, 256 * part + 256)
                summed[lanes, :] = lax.dot_general(
                    left[:, lanes], right_i[...], (((0,), (0,)), ((), ())),
                    preferred_element_type=jnp.float32,
                )
                for g in range(2):
                    slots = range(4 * g, 4 * g + 4)
                    turn_sums(
                        u, [8 * part + k for k in slots],
                        [256 * part + (y_at[k % 2] * 4 + z_part[part][k // 2] // 2) * BLK for k in slots],
                    )
                for k, e in far_first(range(8), (3.5, 2.5, 1.5, 0.5)):
                    own = odd[part] == 0 if (k, e) == (LAST, 0) else None
                    send_sums(u, 8 * part + k, row_part[part][k], e, own)

        wait_sums(u)

        def sums(k):
            return recv3[u, k].astype(jnp.float32)

        total = jnp.zeros((SUB, 128), jnp.float32)
        for k in range(ROWS):
            total += jnp.sum(sums(k), axis=0)
        middle = total * (1.0 / CH)
        total = jnp.zeros((SUB, 128), jnp.float32)
        for k in range(ROWS):
            centred = sums(k) - middle
            total += jnp.sum(centred * centred, axis=0)
        scale = lax.rsqrt(total * (1.0 / CH) + 1e-05)
        for k in range(ROWS):
            centred = sums(k) - middle
            hidden[64 * k : 64 * k + 64, :] = (centred * scale).reshape(64, 128)
        for s in range(SUB):
            hidden_t[:, s * 128 : (s + 1) * 128] = hidden[pl.ds(s, CH, stride=SUB), :].astype(jnp.bfloat16)
        for j in range(4):
            cols = slice(256 * j, 256 * (j + 1))
            update = jnp.dot(final_t[u], hidden_t[:, cols], preferred_element_type=jnp.float32)
            result = pair_t[:, cols] + gate[:, cols] * update
            pair_t[:, cols] = result.astype(jnp.bfloat16).astype(jnp.float32)

    for s in range(SUB):
        block = pair_t[:, s * 128 : (s + 1) * 128].T.astype(jnp.bfloat16)
        for q in range(4):
            out_ref[8 * q + s] = block[32 * q : 32 * q + 32]

    for u in range(2):
        for d in range(ROWS):
            count = 7 if d == SELF else 8
            remote(
                send1.at[u, d, pl.ds(0, count)], send1.at[u, d, pl.ds(0, count)],
                s1.at[u, d], r1.at[u, 0], sibling,
            ).wait_send()
        for g in range(CHUNKS):
            forward1(u, g).wait_send()
        for slot in range(ROWS):
            count = 7 if slot in ((SELF,), (LAST, 8 + LAST))[u] else 8
            block = send3.at[u, slot, pl.ds(0, count)]
            remote(block, block, s3.at[u, slot], r3.at[u], sibling).wait_send()
    remote(send3.at[1, 0, 0], send3.at[1, 0, 0], sx, r3.at[1], sibling).wait_send()


def shards(pair_act, residue_mask, *weights):
    bf16, f32 = jnp.bfloat16, jnp.float32
    dma = pltpu.SemaphoreType.DMA
    vmem = pl.BlockSpec(memory_space=pltpu.VMEM)
    return pl.pallas_call(
        kernel,
        out_shape=jax.ShapeDtypeStruct(pair_act.shape, pair_act.dtype),
        in_specs=[pl.BlockSpec(memory_space=pl.ANY)] * 6,
        out_specs=vmem,
        scratch_shapes=[
            pltpu.SMEM(residue_mask.shape, jnp.int32),
            pltpu.VMEM(pair_act.shape, bf16),
            pltpu.VMEM((2, CH, 5 * CH), bf16),
            pltpu.VMEM((2, CH, CH), bf16),
            pltpu.VMEM((CH, 1024), f32),
            pltpu.VMEM((2, 5 * CH, CH), bf16),
            pltpu.VMEM((2, CH, CH), bf16),
            pltpu.VMEM((SUB, 128), f32),
            pltpu.VMEM((CH, 1024), bf16),
            pltpu.VMEM((5 * CH, 1024), f32),
            pltpu.VMEM((CH, 1024), f32),
            pltpu.VMEM((2, 128, 128), f32),
            pltpu.VMEM((2, ROWS, 8, 2, SUB, 128), bf16),
            pltpu.VMEM((2, 2, CHUNKS, PER, 8, 2, SUB, 128), bf16),
            pltpu.VMEM((512, 512), bf16),
            pltpu.VMEM((256, 512), bf16),
            pltpu.VMEM((512, 256), bf16),
            pltpu.VMEM((512, 256), f32),
            pltpu.VMEM((2, ROWS, 8, SUB, 128), bf16),
            pltpu.VMEM((2, ROWS, 8, SUB, 128), bf16),
            pltpu.VMEM((1024, 128), f32),
            pltpu.VMEM((CH, 1024), bf16),
            dma((6,)),
            dma((2, ROWS)), dma((2, CHUNKS)),
            dma((2, CHUNKS)), dma((2, CHUNKS)),
            dma((2, ROWS)), dma((2,)), dma,
        ],
        compiler_params=pltpu.CompilerParams(
            collective_id=0, has_side_effects=True, vmem_limit_bytes=60 * 1024 * 1024
        ),
    )(residue_mask, pair_act, *weights)


def solution(mesh):
    return jax.shard_map(
        shards,
        mesh=mesh,
        in_specs=(P("row", "col", None), P(), P(), P(), P(), P()),
        out_specs=P("row", "col", None),
        check_vma=False,
    )
```

```python
import jax
import jax.numpy as jnp
from jax import lax
from jax.experimental import pallas as pl
from jax.experimental.pallas import tpu as pltpu
from jax.sharding import PartitionSpec as P

ROWS = 16
COLS = 16
CH = 128
BLK = 32
SUB = 8
CHUNKS = 4
PER = ROWS // CHUNKS
STEPS = (4, 3, -3, 2, -2, 1, -1, 0)
SELF = 2 * STEPS.index(0)
EVEN, ODD = (4, 2, -2, 0), (3, -3, 1, -1)
LAST = 2 * EVEN.index(0)
MESH = pl.DeviceIdType.MESH


def far_first(slots, steps=STEPS):
    def hops(to):
        d, e = to
        return abs(steps[d // 2]) + (0, 1, 2, 1)[e // 2] + ((0, 2), (1, 1))[d % 2][e % 2]

    return sorted(((d, e) for d in slots for e in range(8)), key=hops, reverse=True)


def block_transpose(parts):
    lane = lax.broadcasted_iota(jnp.int32, parts[0].shape, 1)
    low = lane < 64
    even = (lane // 32) % 2 == 0
    t0, t1, t2, t3 = parts
    u0 = jnp.where(low, t0, pltpu.roll(t2, 64, 1))
    u2 = jnp.where(low, pltpu.roll(t0, 64, 1), t2)
    u1 = jnp.where(low, t1, pltpu.roll(t3, 64, 1))
    u3 = jnp.where(low, pltpu.roll(t1, 64, 1), t3)
    return (
        jnp.where(even, u0, pltpu.roll(u1, 32, 1)),
        jnp.where(even, pltpu.roll(u0, 96, 1), u1),
        jnp.where(even, u2, pltpu.roll(u3, 32, 1)),
        jnp.where(even, pltpu.roll(u2, 96, 1), u3),
    )


def kernel(
    mask_hbm, pair_hbm, w_out, f_out, w_in, f_in, out_ref,
    mask_ref, pair_ref, w_ref, f_ref,
    pair_t, weights_t, final_t, half_mask, normed, mixed, gate, stage,
    send1, recv1, left, right_o, right_i, summed, send3, recv3,
    hidden, hidden_t,
    s0, s1, r1, sf, rf, s3, r3, sx, halves, sh, rh, fs, fr,
):
    loads = [
        pltpu.make_async_copy(src, dst, s0.at[i])
        for i, (src, dst) in enumerate(
            (
                (pair_hbm, pair_ref), (w_out, w_ref.at[0]), (mask_hbm, mask_ref),
                (w_in, w_ref.at[1]), (f_out, f_ref.at[0]), (f_in, f_ref.at[1]),
            )
        )
    ]
    for load in loads:
        load.start()

    row, col = lax.axis_index("row"), lax.axis_index("col")
    y_lo, z = row // 8, row % 8
    x, y_hi, core = col // 4, (col // 2) % 2, col % 2
    chip = col // 2
    z_to = [(z + b + 8) % 8 for b in STEPS]
    z_from = [(z + 8 - b) % 8 for b in STEPS]
    y_at = [y_lo, 1 - y_lo]
    core_at = [core, 1 - core]
    x_at = [(x + e) % 4 for e in range(4)]
    y_hi_at = [y_hi, 1 - y_hi]
    row_to = [y_at[d % 2] * 8 + z_to[d // 2] for d in range(ROWS)]
    odd = [(z + core) % 2, (z + core + 1) % 2]
    z_part = [
        [(z + 8 + EVEN[j] + odd[part] * (ODD[j] - EVEN[j])) % 8 for j in range(4)] for part in range(2)
    ]
    row_part = [[y_at[k % 2] * 8 + z_part[part][k // 2] for k in range(8)] for part in range(2)]
    row_from = [y_at[d % 2] * 8 + z_from[d // 2] for d in range(ROWS)]
    chip_to = [x_at[e // 2] * 2 + y_hi_at[e % 2] for e in range(8)]
    col_to = [chip_to[e] * 2 + core for e in range(8)]
    sibling = {"col": chip * 2 + 1 - core}

    barrier = pltpu.get_barrier_semaphore()
    for d in range(ROWS):
        for e in range(8):
            if (d, e) != (SELF, 0):
                pl.semaphore_signal(
                    barrier, inc=1, device_id={"row": row_to[d], "col": col_to[e]}, device_id_type=MESH
                )
    pl.semaphore_signal(barrier, inc=1, device_id=sibling, device_id_type=MESH)

    def remote(src, dst, ssem, rsem, to):
        return pltpu.make_async_remote_copy(
            src_ref=src, dst_ref=dst, send_sem=ssem, recv_sem=rsem,
            device_id=to, device_id_type=MESH,
        )

    def copy1(u, d, e):
        src = send1.at[u, d, chip_to[e]]
        dst = recv1.at[u, core, d // PER, d % PER, chip]
        if (d, e) == (SELF, 0):
            return pltpu.make_async_copy(src, dst, r1.at[u, d // PER])
        return remote(
            src, dst, s1.at[u, d], r1.at[u, d // PER], {"row": row_to[d], "col": col_to[e]}
        )

    def send_side(side, d, e):
        src = send1.at[0, d, chip_to[e], side]
        dst = halves.at[side, core, d // PER, d % PER, chip]
        sem = rh.at[4 if side else d // PER]
        if (d, e) == (SELF, 0):
            pltpu.make_async_copy(src, dst, sem).start()
        else:
            to = {"row": row_to[d], "col": col_to[e]}
            remote(src, dst, sh.at[side, d], sem, to).start()

    def wait_side(side, g):
        block = halves.at[1, core] if side else halves.at[0, core, g]
        remote(block, block, sx, rh.at[4 if side else g], sibling).wait_recv()

    def forward_side(side, g):
        block = halves.at[1, core] if side else halves.at[0, core, g]
        at = 4 if side else g
        return remote(block, block, fs.at[at], fr.at[at], sibling)

    def wait1(u, g):
        block = recv1.at[u, core, g]
        remote(block, block, sx, r1.at[u, g], sibling).wait_recv()

    def forward1(u, g):
        block = recv1.at[u, core, g, :, :, 0]
        return remote(block, block, sf.at[u, g], rf.at[u, g], sibling)

    def send_sums(u, slot, to_row, e, own):
        src, dst = send3.at[u, slot, chip_to[e]], recv3.at[u, row, chip]
        to = {"row": to_row, "col": col_to[e]}

        def here():
            pltpu.make_async_copy(src, dst, r3.at[u]).start()

        if own is None:
            remote(src, dst, s3.at[u, slot], r3.at[u], to).start()
        elif own is True:
            here()
        else:
            pl.when(own)(here)

            @pl.when(jnp.logical_not(own))
            def _():
                remote(src, dst, sx, r3.at[u], to).start()

    def wait_sums(u):
        block = recv3.at[u]
        remote(block, block, sx, r3.at[u], sibling).wait_recv()

    def turn_weights(u):
        weights_t[u] = w_ref[u].astype(jnp.float32).T.astype(jnp.bfloat16)

    loads[0].wait()
    for s in range(SUB):
        block = jnp.concatenate([pair_ref[8 * q + s] for q in range(4)], axis=0)
        pair_t[:, s * 128 : (s + 1) * 128] = block.astype(jnp.float32).T
    loads[1].wait()
    turn_weights(0)

    loads[2].wait()
    lane = lax.broadcasted_iota(jnp.int32, (SUB, 128), 1)
    sub = lax.broadcasted_iota(jnp.int32, (SUB, 128), 0)
    by_row = jnp.zeros((SUB, 128), jnp.float32)
    by_col = jnp.zeros((SUB, 128), jnp.float32)
    for k in range(BLK):
        by_col = jnp.where(lane % 32 == k, mask_ref[col * BLK + k].astype(jnp.float32), by_col)
        by_row = jnp.where(
            (lane // 32) * 8 + sub == k, mask_ref[row * BLK + k].astype(jnp.float32), by_row
        )
    half_mask[...] = 0.5 * by_row * by_col

    def project(u):
        for j in range(4):
            cols = slice(256 * j, 256 * (j + 1))
            values = pair_t[:, cols]
            middle = jnp.mean(values, axis=0, keepdims=True)
            centred = values - middle
            spread = jnp.mean(centred * centred, axis=0, keepdims=True)
            normed[:, cols] = (centred * lax.rsqrt(spread + 1e-05)).astype(jnp.bfloat16)
            mixed[:, cols] = jnp.dot(
                weights_t[u], normed[:, cols], preferred_element_type=jnp.float32
            )

    def sides(u, d):
        at = row_to[d] * 8
        held = stage.at[d % 2]

        def part(k):
            return mixed[pl.ds(pl.multiple_of(at + k * CH, 8), 8), :]

        for side in range(2):
            value, gates = part(2 * side), part(2 * side + 1)
            for s in range(SUB):
                cols = slice(s * 128, (s + 1) * 128)
                held[pl.ds(side * 8 + s, 8, stride=16), :] = (
                    (jnp.tanh(0.5 * gates[:, cols]) + 1.0) * value[:, cols] * half_mask[s : s + 1, :]
                )
        return held[...].astype(jnp.bfloat16).reshape(8, 2, SUB, 128)

    def turned_tiles(tile, slots, v):
        turned = block_transpose(
            [jnp.concatenate([tile(i, 4 * v + t) for i in slots], axis=0) for t in range(4)]
        )
        return [
            jnp.concatenate([w[8 * i : 8 * i + 8] for w in turned], axis=0)
            for i in range(len(slots))
        ]

    def band(r):
        return pl.ds(pl.multiple_of(r * BLK, BLK), BLK)

    def assemble_left(g, part):
        for v in range(2):
            lanes = slice(256 * part + 128 * v, 256 * part + 128 * v + 128)
            tile = lambda i, p: halves[0, core_at[part], g, i, p]
            for i, rows in enumerate(turned_tiles(tile, range(PER), v)):
                left[(PER * g + i) * BLK : (PER * g + i + 1) * BLK, lanes] = rows

    def assemble_right(g, part):
        step = (z + core + g) % 2
        z_src = z_from[2 * g] + step * (z_from[2 * g + 1] - z_from[2 * g])
        for v in range(2):
            lanes = slice(256 * part + 128 * v, 256 * part + 128 * v + 128)
            tile = lambda i, p: halves[1, core_at[part], g, i, p]
            for a, rows in enumerate(turned_tiles(tile, [2 * step + a for a in range(2)], v)):
                right_o[band(y_at[a] * 4 + z_src // 2), lanes] = rows

    def finish_rows(g):
        forward_side(0, g).wait_recv()
        assemble_left(g, 1)
        rows = slice(128 * g, 128 * g + 128)
        summed[rows, :] = lax.dot_general(
            left[rows, :], right_o[...], (((1,), (1,)), ((), ())), preferred_element_type=jnp.float32
        )
        slots = range(PER * g, PER * g + PER)
        turn_sums(0, slots, [d * BLK for d in slots])
        for d, e in far_first(slots):
            send_sums(0, d, row_from[d], e, True if (d, e) == (SELF, 0) else None)

    def assemble(g, part):
        for v in range(2):
            lanes = slice(256 * part + 128 * v, 256 * part + 128 * v + 128)
            for side in range(2 - part):
                tile = lambda i, p: recv1[1, core_at[part], g, i, p, side]
                for i, rows in enumerate(turned_tiles(tile, range(PER), v)):
                    (left, right_i)[side][band(row_from[g * PER + i]), lanes] = rows

    def turn_sums(u, slots, at):
        for v in range(2):
            turned = block_transpose(
                [
                    jnp.concatenate(
                        [
                            summed[pl.ds(pl.multiple_of(a + 8 * q, 8), 8), 128 * v : 128 * v + 128]
                            for a in at
                        ],
                        axis=0,
                    )
                    for q in range(4)
                ]
            )
            for t, tiles in enumerate(turned):
                for i, slot in enumerate(slots):
                    send3[u, slot, 4 * v + t] = tiles[8 * i : 8 * i + 8].astype(jnp.bfloat16)

    for u in range(2):
        project(u)
        if u == 0:
            for d in range(ROWS):
                send1[u, d] = sides(u, d)
            pl.semaphore_wait(barrier, 128)

        if u == 0:
            for d, e in far_first(range(ROWS)):
                send_side(1, d, e)
        for g in range(CHUNKS):
            slots = range(g * PER, (g + 1) * PER)
            if u == 1:
                for d in slots:
                    send1[u, d] = sides(u, d)
            for d, e in far_first(slots):
                if u == 0:
                    send_side(0, d, e)
                else:
                    copy1(u, d, e).start()

        gate[...] = 0.5 * jnp.tanh(0.5 * mixed[4 * CH :, :]) + 0.5
        if u == 0:
            for load in loads[3:]:
                load.wait()
            turn_weights(1)
            for k in range(2):
                final_t[k] = f_ref[k].astype(jnp.float32).T.astype(jnp.bfloat16)

        if u == 0:
            wait_side(1, 0)
            forward_side(1, 0).start()
            for g in range(CHUNKS):
                assemble_right(g, 0)
            for g in range(CHUNKS):
                wait_side(0, g)
                forward_side(0, g).start()
                assemble_left(g, 0)
                if g == 0:
                    forward_side(1, 0).wait_recv()
                    for k in range(CHUNKS):
                        assemble_right(k, 1)
                else:
                    finish_rows(g - 1)
            finish_rows(CHUNKS - 1)
        else:
            for g in range(CHUNKS):
                wait1(u, g)
                forward1(u, g).start()
                assemble(g, 0)
            for part in range(2):
                if part == 1:
                    for g in range(CHUNKS):
                        forward1(u, g).wait_recv()
                        assemble(g, 1)
                lanes = slice(256 * part, 256 * part + 256)
                summed[lanes, :] = lax.dot_general(
                    left[:, lanes], right_i[...], (((0,), (0,)), ((), ())),
                    preferred_element_type=jnp.float32,
                )
                for g in range(2):
                    slots = range(4 * g, 4 * g + 4)
                    turn_sums(
                        u, [8 * part + k for k in slots],
                        [256 * part + (y_at[k % 2] * 4 + z_part[part][k // 2] // 2) * BLK for k in slots],
                    )
                for k, e in far_first(range(8), (3.5, 2.5, 1.5, 0.5)):
                    own = odd[part] == 0 if (k, e) == (LAST, 0) else None
                    send_sums(u, 8 * part + k, row_part[part][k], e, own)

        wait_sums(u)

        def sums(k):
            return recv3[u, k].astype(jnp.float32)

        total = jnp.zeros((SUB, 128), jnp.float32)
        for k in range(ROWS):
            total += jnp.sum(sums(k), axis=0)
        middle = total * (1.0 / CH)
        total = jnp.zeros((SUB, 128), jnp.float32)
        for k in range(ROWS):
            centred = sums(k) - middle
            total += jnp.sum(centred * centred, axis=0)
        scale = lax.rsqrt(total * (1.0 / CH) + 1e-05)
        for k in range(ROWS):
            centred = sums(k) - middle
            hidden[64 * k : 64 * k + 64, :] = (centred * scale).reshape(64, 128)
        for s in range(SUB):
            hidden_t[:, s * 128 : (s + 1) * 128] = hidden[pl.ds(s, CH, stride=SUB), :].astype(jnp.bfloat16)
        for j in range(4):
            cols = slice(256 * j, 256 * (j + 1))
            update = jnp.dot(final_t[u], hidden_t[:, cols], preferred_element_type=jnp.float32)
            result = pair_t[:, cols] + gate[:, cols] * update
            pair_t[:, cols] = result.astype(jnp.bfloat16).astype(jnp.float32)

    for s in range(SUB):
        block = pair_t[:, s * 128 : (s + 1) * 128].T.astype(jnp.bfloat16)
        for q in range(4):
            out_ref[8 * q + s] = block[32 * q : 32 * q + 32]

    for d in range(ROWS):
        count = 7 if d == SELF else 8
        for side in range(2):
            block = send1.at[0, d, pl.ds(0, count), side]
            remote(block, block, sh.at[side, d], rh.at[0], sibling).wait_send()
        block = send1.at[1, d, pl.ds(0, count)]
        remote(block, block, s1.at[1, d], r1.at[1, 0], sibling).wait_send()
    for g in range(CHUNKS):
        forward_side(0, g).wait_send()
        forward1(1, g).wait_send()
    forward_side(1, 0).wait_send()
    for u in range(2):
        for slot in range(ROWS):
            count = 7 if slot in ((SELF,), (LAST, 8 + LAST))[u] else 8
            block = send3.at[u, slot, pl.ds(0, count)]
            remote(block, block, s3.at[u, slot], r3.at[u], sibling).wait_send()
    remote(send3.at[1, 0, 0], send3.at[1, 0, 0], sx, r3.at[1], sibling).wait_send()


def shards(pair_act, residue_mask, *weights):
    bf16, f32 = jnp.bfloat16, jnp.float32
    dma = pltpu.SemaphoreType.DMA
    vmem = pl.BlockSpec(memory_space=pltpu.VMEM)
    return pl.pallas_call(
        kernel,
        out_shape=jax.ShapeDtypeStruct(pair_act.shape, pair_act.dtype),
        in_specs=[pl.BlockSpec(memory_space=pl.ANY)] * 6,
        out_specs=vmem,
        scratch_shapes=[
            pltpu.SMEM(residue_mask.shape, jnp.int32),
            pltpu.VMEM(pair_act.shape, bf16),
            pltpu.VMEM((2, CH, 5 * CH), bf16),
            pltpu.VMEM((2, CH, CH), bf16),
            pltpu.VMEM((CH, 1024), f32),
            pltpu.VMEM((2, 5 * CH, CH), bf16),
            pltpu.VMEM((2, CH, CH), bf16),
            pltpu.VMEM((SUB, 128), f32),
            pltpu.VMEM((CH, 1024), bf16),
            pltpu.VMEM((5 * CH, 1024), f32),
            pltpu.VMEM((CH, 1024), f32),
            pltpu.VMEM((2, 128, 128), f32),
            pltpu.VMEM((2, ROWS, 8, 2, SUB, 128), bf16),
            pltpu.VMEM((2, 2, CHUNKS, PER, 8, 2, SUB, 128), bf16),
            pltpu.VMEM((512, 512), bf16),
            pltpu.VMEM((256, 512), bf16),
            pltpu.VMEM((512, 256), bf16),
            pltpu.VMEM((512, 256), f32),
            pltpu.VMEM((2, ROWS, 8, SUB, 128), bf16),
            pltpu.VMEM((2, ROWS, 8, SUB, 128), bf16),
            pltpu.VMEM((1024, 128), f32),
            pltpu.VMEM((CH, 1024), bf16),
            dma((6,)),
            dma((2, ROWS)), dma((2, CHUNKS)),
            dma((2, CHUNKS)), dma((2, CHUNKS)),
            dma((2, ROWS)), dma((2,)), dma,
            pltpu.VMEM((2, 2, CHUNKS, PER, 8, SUB, 128), bf16),
            dma((2, ROWS)), dma((5,)), dma((5,)), dma((5,)),
        ],
        compiler_params=pltpu.CompilerParams(
            collective_id=0, has_side_effects=True, vmem_limit_bytes=60 * 1024 * 1024
        ),
    )(residue_mask, pair_act, *weights)


def solution(mesh):
    return jax.shard_map(
        shards,
        mesh=mesh,
        in_specs=(P("row", "col", None), P(), P(), P(), P(), P()),
        out_specs=P("row", "col", None),
        check_vma=False,
    )
```

```python
import jax
import jax.numpy as jnp
from jax import lax
from jax.experimental import pallas as pl
from jax.experimental.pallas import tpu as pltpu
from jax.sharding import PartitionSpec as P

ROWS = 16
COLS = 16
CH = 128
BLK = 32
SUB = 8
CHUNKS = 4
PER = ROWS // CHUNKS
STEPS = (4, 3, -3, 2, -2, 1, -1, 0)
SELF = 2 * STEPS.index(0)
EVEN, ODD = (4, 2, -2, 0), (3, -3, 1, -1)
LAST = 2 * EVEN.index(0)
MESH = pl.DeviceIdType.MESH


def far_first(slots, steps=STEPS):
    def hops(to):
        d, e = to
        return abs(steps[d // 2]) + (0, 1, 2, 1)[e // 2] + ((0, 2), (1, 1))[d % 2][e % 2]

    return sorted(((d, e) for d in slots for e in range(8)), key=hops, reverse=True)


def block_transpose(parts):
    lane = lax.broadcasted_iota(jnp.int32, parts[0].shape, 1)
    low = lane < 64
    even = (lane // 32) % 2 == 0
    t0, t1, t2, t3 = parts
    u0 = jnp.where(low, t0, pltpu.roll(t2, 64, 1))
    u2 = jnp.where(low, pltpu.roll(t0, 64, 1), t2)
    u1 = jnp.where(low, t1, pltpu.roll(t3, 64, 1))
    u3 = jnp.where(low, pltpu.roll(t1, 64, 1), t3)
    return (
        jnp.where(even, u0, pltpu.roll(u1, 32, 1)),
        jnp.where(even, pltpu.roll(u0, 96, 1), u1),
        jnp.where(even, u2, pltpu.roll(u3, 32, 1)),
        jnp.where(even, pltpu.roll(u2, 96, 1), u3),
    )


def kernel(
    mask_hbm, pair_hbm, w_out, f_out, w_in, f_in, out_ref,
    mask_ref, pair_ref, w_ref, f_ref,
    pair_t, weights_t, final_t, half_mask, normed, mixed, gate, stage,
    send1, recv1, left, right_o, right_i, summed, send3, recv3,
    hidden, hidden_t,
    s0, s1, r1, sf, rf, s3, r3, sx, halves, sh, rh, fs, fr,
):
    loads = [
        pltpu.make_async_copy(src, dst, s0.at[i])
        for i, (src, dst) in enumerate(
            (
                (pair_hbm, pair_ref), (w_out, w_ref.at[0]), (mask_hbm, mask_ref),
                (w_in, w_ref.at[1]), (f_out, f_ref.at[0]), (f_in, f_ref.at[1]),
            )
        )
    ]
    for load in loads:
        load.start()

    row, col = lax.axis_index("row"), lax.axis_index("col")
    y_lo, z = row // 8, row % 8
    x, y_hi, core = col // 4, (col // 2) % 2, col % 2
    chip = col // 2
    z_to = [(z + b + 8) % 8 for b in STEPS]
    z_from = [(z + 8 - b) % 8 for b in STEPS]
    y_at = [y_lo, 1 - y_lo]
    core_at = [core, 1 - core]
    x_at = [(x + e) % 4 for e in range(4)]
    y_hi_at = [y_hi, 1 - y_hi]
    row_to = [y_at[d % 2] * 8 + z_to[d // 2] for d in range(ROWS)]
    odd = [(z + core) % 2, (z + core + 1) % 2]
    z_part = [
        [(z + 8 + EVEN[j] + odd[part] * (ODD[j] - EVEN[j])) % 8 for j in range(4)] for part in range(2)
    ]
    row_part = [[y_at[k % 2] * 8 + z_part[part][k // 2] for k in range(8)] for part in range(2)]
    row_from = [y_at[d % 2] * 8 + z_from[d // 2] for d in range(ROWS)]
    chip_to = [x_at[e // 2] * 2 + y_hi_at[e % 2] for e in range(8)]
    col_to = [chip_to[e] * 2 + core for e in range(8)]
    sibling = {"col": chip * 2 + 1 - core}

    barrier = pltpu.get_barrier_semaphore()
    for d in range(ROWS):
        for e in range(8):
            if (d, e) != (SELF, 0):
                pl.semaphore_signal(
                    barrier, inc=1, device_id={"row": row_to[d], "col": col_to[e]}, device_id_type=MESH
                )
    pl.semaphore_signal(barrier, inc=1, device_id=sibling, device_id_type=MESH)

    def remote(src, dst, ssem, rsem, to):
        return pltpu.make_async_remote_copy(
            src_ref=src, dst_ref=dst, send_sem=ssem, recv_sem=rsem,
            device_id=to, device_id_type=MESH,
        )

    def copy1(u, d, e):
        src = send1.at[u, d, chip_to[e]]
        dst = recv1.at[u, core, d // PER, d % PER, chip]
        if (d, e) == (SELF, 0):
            return pltpu.make_async_copy(src, dst, r1.at[u, d // PER])
        return remote(
            src, dst, s1.at[u, d], r1.at[u, d // PER], {"row": row_to[d], "col": col_to[e]}
        )

    def send_side(side, d, e):
        src = send1.at[0, d, chip_to[e], side]
        dst = halves.at[side, core, d // PER, d % PER, chip]
        sem = rh.at[4 if side else d // PER]
        if (d, e) == (SELF, 0):
            pltpu.make_async_copy(src, dst, sem).start()
        else:
            to = {"row": row_to[d], "col": col_to[e]}
            remote(src, dst, sh.at[side, d], sem, to).start()

    def wait_side(side, g):
        block = halves.at[1, core] if side else halves.at[0, core, g]
        remote(block, block, sx, rh.at[4 if side else g], sibling).wait_recv()

    def forward_side(side, g):
        block = halves.at[1, core] if side else halves.at[0, core, g]
        at = 4 if side else g
        return remote(block, block, fs.at[at], fr.at[at], sibling)

    def wait1(u, g):
        block = recv1.at[u, core, g]
        remote(block, block, sx, r1.at[u, g], sibling).wait_recv()

    def forward1(u, g):
        block = recv1.at[u, core, g, :, :, 0]
        return remote(block, block, sf.at[u, g], rf.at[u, g], sibling)

    def send_sums(u, slot, to_row, e, own):
        src, dst = send3.at[u, slot, chip_to[e]], recv3.at[u, row, chip]
        to = {"row": to_row, "col": col_to[e]}

        def here():
            pltpu.make_async_copy(src, dst, r3.at[u]).start()

        if own is None:
            remote(src, dst, s3.at[u, slot], r3.at[u], to).start()
        elif own is True:
            here()
        else:
            pl.when(own)(here)

            @pl.when(jnp.logical_not(own))
            def _():
                remote(src, dst, sx, r3.at[u], to).start()

    def wait_sums(u):
        block = recv3.at[u]
        remote(block, block, sx, r3.at[u], sibling).wait_recv()

    def turn_weights(u):
        weights_t[u] = w_ref[u].astype(jnp.float32).T.astype(jnp.bfloat16)

    loads[0].wait()
    for s in range(SUB):
        block = jnp.concatenate([pair_ref[8 * q + s] for q in range(4)], axis=0)
        pair_t[:, s * 128 : (s + 1) * 128] = block.astype(jnp.float32).T
    loads[1].wait()
    turn_weights(0)

    loads[2].wait()
    lane = lax.broadcasted_iota(jnp.int32, (SUB, 128), 1)
    sub = lax.broadcasted_iota(jnp.int32, (SUB, 128), 0)
    by_row = jnp.zeros((SUB, 128), jnp.float32)
    by_col = jnp.zeros((SUB, 128), jnp.float32)
    for k in range(BLK):
        by_col = jnp.where(lane % 32 == k, mask_ref[col * BLK + k].astype(jnp.float32), by_col)
        by_row = jnp.where(
            (lane // 32) * 8 + sub == k, mask_ref[row * BLK + k].astype(jnp.float32), by_row
        )
    half_mask[...] = 0.5 * by_row * by_col

    def project(u):
        for j in range(4):
            cols = slice(256 * j, 256 * (j + 1))
            values = pair_t[:, cols]
            middle = jnp.mean(values, axis=0, keepdims=True)
            centred = values - middle
            spread = jnp.mean(centred * centred, axis=0, keepdims=True)
            normed[:, cols] = (centred * lax.rsqrt(spread + 1e-05)).astype(jnp.bfloat16)
            mixed[:, cols] = jnp.dot(
                weights_t[u], normed[:, cols], preferred_element_type=jnp.float32
            )

    def sides(u, d):
        at = row_to[d] * 8
        held = stage.at[d % 2]

        def part(k):
            return mixed[pl.ds(pl.multiple_of(at + k * CH, 8), 8), :]

        for side in range(2):
            value, gates = part(2 * side), part(2 * side + 1)
            for s in range(SUB):
                cols = slice(s * 128, (s + 1) * 128)
                held[pl.ds(side * 8 + s, 8, stride=16), :] = (
                    (jnp.tanh(0.5 * gates[:, cols]) + 1.0) * value[:, cols] * half_mask[s : s + 1, :]
                )
        return held[...].astype(jnp.bfloat16).reshape(8, 2, SUB, 128)

    def turned_tiles(tile, slots, v):
        turned = block_transpose(
            [jnp.concatenate([tile(i, 4 * v + t) for i in slots], axis=0) for t in range(4)]
        )
        return [
            jnp.concatenate([w[8 * i : 8 * i + 8] for w in turned], axis=0)
            for i in range(len(slots))
        ]

    def band(r):
        return pl.ds(pl.multiple_of(r * BLK, BLK), BLK)

    def assemble_left(g, part):
        for v in range(2):
            lanes = slice(256 * part + 128 * v, 256 * part + 128 * v + 128)
            tile = lambda i, p: halves[0, core_at[part], g, i, p]
            for i, rows in enumerate(turned_tiles(tile, range(PER), v)):
                left[(PER * g + i) * BLK : (PER * g + i + 1) * BLK, lanes] = rows

    def assemble_right(g, part):
        step = (z + core + g) % 2
        z_src = z_from[2 * g] + step * (z_from[2 * g + 1] - z_from[2 * g])
        for v in range(2):
            lanes = slice(256 * part + 128 * v, 256 * part + 128 * v + 128)
            tile = lambda i, p: halves[1, core_at[part], g, i, p]
            for a, rows in enumerate(turned_tiles(tile, [2 * step + a for a in range(2)], v)):
                right_o[band(y_at[a] * 4 + z_src // 2), lanes] = rows

    def finish_rows(g):
        forward_side(0, g).wait_recv()
        assemble_left(g, 1)
        rows = slice(128 * g, 128 * g + 128)
        summed[rows, :] = lax.dot_general(
            left[rows, :], right_o[...], (((1,), (1,)), ((), ())), preferred_element_type=jnp.float32
        )
        slots = range(PER * g, PER * g + PER)
        turn_sums(0, slots, [d * BLK for d in slots])
        for d, e in far_first(slots):
            send_sums(0, d, row_from[d], e, True if (d, e) == (SELF, 0) else None)

    def assemble(g, part):
        for v in range(2):
            lanes = slice(256 * part + 128 * v, 256 * part + 128 * v + 128)
            for side in range(2 - part):
                tile = lambda i, p: recv1[1, core_at[part], g, i, p, side]
                for i, rows in enumerate(turned_tiles(tile, range(PER), v)):
                    (left, right_i)[side][band(row_from[g * PER + i]), lanes] = rows

    def turn_sums(u, slots, at):
        for v in range(2):
            turned = block_transpose(
                [
                    jnp.concatenate(
                        [
                            summed[pl.ds(pl.multiple_of(a + 8 * q, 8), 8), 128 * v : 128 * v + 128]
                            for a in at
                        ],
                        axis=0,
                    )
                    for q in range(4)
                ]
            )
            for t, tiles in enumerate(turned):
                for i, slot in enumerate(slots):
                    send3[u, slot, 4 * v + t] = tiles[8 * i : 8 * i + 8].astype(jnp.bfloat16)

    for u in range(2):
        project(u)
        if u == 0:
            for d in range(ROWS):
                send1[u, d] = sides(u, d)
            pl.semaphore_wait(barrier, 128)

        if u == 0:
            for d, e in far_first(range(ROWS)):
                send_side(1, d, e)
            for g in range(CHUNKS):
                for d, e in far_first(range(g * PER, (g + 1) * PER)):
                    send_side(0, d, e)
        else:
            for slots in (range(1), range(1, 2), range(2, 4), range(4, 8), range(8, 16)):
                for d in slots:
                    send1[u, d] = sides(u, d)
                for d, e in far_first(slots):
                    copy1(u, d, e).start()

        gate[...] = 0.5 * jnp.tanh(0.5 * mixed[4 * CH :, :]) + 0.5
        if u == 0:
            for load in loads[3:]:
                load.wait()
            turn_weights(1)
            for k in range(2):
                final_t[k] = f_ref[k].astype(jnp.float32).T.astype(jnp.bfloat16)

        if u == 0:
            wait_side(1, 0)
            forward_side(1, 0).start()
            for g in range(CHUNKS):
                assemble_right(g, 0)
            for g in range(CHUNKS):
                wait_side(0, g)
                forward_side(0, g).start()
                assemble_left(g, 0)
                if g == 0:
                    forward_side(1, 0).wait_recv()
                    for k in range(CHUNKS):
                        assemble_right(k, 1)
                else:
                    finish_rows(g - 1)
            finish_rows(CHUNKS - 1)
        else:
            for g in range(CHUNKS):
                wait1(u, g)
                forward1(u, g).start()
                assemble(g, 0)
            for part in range(2):
                if part == 1:
                    for g in range(CHUNKS):
                        forward1(u, g).wait_recv()
                        assemble(g, 1)
                lanes = slice(256 * part, 256 * part + 256)
                summed[lanes, :] = lax.dot_general(
                    left[:, lanes], right_i[...], (((0,), (0,)), ((), ())),
                    preferred_element_type=jnp.float32,
                )
                for g in range(2):
                    slots = range(4 * g, 4 * g + 4)
                    turn_sums(
                        u, [8 * part + k for k in slots],
                        [256 * part + (y_at[k % 2] * 4 + z_part[part][k // 2] // 2) * BLK for k in slots],
                    )
                for k, e in far_first(range(8), (3.5, 2.5, 1.5, 0.5)):
                    own = odd[part] == 0 if (k, e) == (LAST, 0) else None
                    send_sums(u, 8 * part + k, row_part[part][k], e, own)

        wait_sums(u)

        def sums(k):
            return recv3[u, k].astype(jnp.float32)

        total = jnp.zeros((SUB, 128), jnp.float32)
        for k in range(ROWS):
            total += jnp.sum(sums(k), axis=0)
        middle = total * (1.0 / CH)
        total = jnp.zeros((SUB, 128), jnp.float32)
        for k in range(ROWS):
            centred = sums(k) - middle
            total += jnp.sum(centred * centred, axis=0)
        scale = lax.rsqrt(total * (1.0 / CH) + 1e-05)
        for k in range(ROWS):
            centred = sums(k) - middle
            hidden[64 * k : 64 * k + 64, :] = (centred * scale).reshape(64, 128)
        for s in range(SUB):
            hidden_t[:, s * 128 : (s + 1) * 128] = hidden[pl.ds(s, CH, stride=SUB), :].astype(jnp.bfloat16)
        for j in range(4):
            cols = slice(256 * j, 256 * (j + 1))
            update = jnp.dot(final_t[u], hidden_t[:, cols], preferred_element_type=jnp.float32)
            result = pair_t[:, cols] + gate[:, cols] * update
            pair_t[:, cols] = result.astype(jnp.bfloat16).astype(jnp.float32)

    for s in range(SUB):
        block = pair_t[:, s * 128 : (s + 1) * 128].T.astype(jnp.bfloat16)
        for q in range(4):
            out_ref[8 * q + s] = block[32 * q : 32 * q + 32]

    for d in range(ROWS):
        count = 7 if d == SELF else 8
        for side in range(2):
            block = send1.at[0, d, pl.ds(0, count), side]
            remote(block, block, sh.at[side, d], rh.at[0], sibling).wait_send()
        block = send1.at[1, d, pl.ds(0, count)]
        remote(block, block, s1.at[1, d], r1.at[1, 0], sibling).wait_send()
    for g in range(CHUNKS):
        forward_side(0, g).wait_send()
        forward1(1, g).wait_send()
    forward_side(1, 0).wait_send()
    for u in range(2):
        for slot in range(ROWS):
            count = 7 if slot in ((SELF,), (LAST, 8 + LAST))[u] else 8
            block = send3.at[u, slot, pl.ds(0, count)]
            remote(block, block, s3.at[u, slot], r3.at[u], sibling).wait_send()
    remote(send3.at[1, 0, 0], send3.at[1, 0, 0], sx, r3.at[1], sibling).wait_send()


def shards(pair_act, residue_mask, *weights):
    bf16, f32 = jnp.bfloat16, jnp.float32
    dma = pltpu.SemaphoreType.DMA
    vmem = pl.BlockSpec(memory_space=pltpu.VMEM)
    return pl.pallas_call(
        kernel,
        out_shape=jax.ShapeDtypeStruct(pair_act.shape, pair_act.dtype),
        in_specs=[pl.BlockSpec(memory_space=pl.ANY)] * 6,
        out_specs=vmem,
        scratch_shapes=[
            pltpu.SMEM(residue_mask.shape, jnp.int32),
            pltpu.VMEM(pair_act.shape, bf16),
            pltpu.VMEM((2, CH, 5 * CH), bf16),
            pltpu.VMEM((2, CH, CH), bf16),
            pltpu.VMEM((CH, 1024), f32),
            pltpu.VMEM((2, 5 * CH, CH), bf16),
            pltpu.VMEM((2, CH, CH), bf16),
            pltpu.VMEM((SUB, 128), f32),
            pltpu.VMEM((CH, 1024), bf16),
            pltpu.VMEM((5 * CH, 1024), f32),
            pltpu.VMEM((CH, 1024), f32),
            pltpu.VMEM((2, 128, 128), f32),
            pltpu.VMEM((2, ROWS, 8, 2, SUB, 128), bf16),
            pltpu.VMEM((2, 2, CHUNKS, PER, 8, 2, SUB, 128), bf16),
            pltpu.VMEM((512, 512), bf16),
            pltpu.VMEM((256, 512), bf16),
            pltpu.VMEM((512, 256), bf16),
            pltpu.VMEM((512, 256), f32),
            pltpu.VMEM((2, ROWS, 8, SUB, 128), bf16),
            pltpu.VMEM((2, ROWS, 8, SUB, 128), bf16),
            pltpu.VMEM((1024, 128), f32),
            pltpu.VMEM((CH, 1024), bf16),
            dma((6,)),
            dma((2, ROWS)), dma((2, CHUNKS)),
            dma((2, CHUNKS)), dma((2, CHUNKS)),
            dma((2, ROWS)), dma((2,)), dma,
            pltpu.VMEM((2, 2, CHUNKS, PER, 8, SUB, 128), bf16),
            dma((2, ROWS)), dma((5,)), dma((5,)), dma((5,)),
        ],
        compiler_params=pltpu.CompilerParams(
            collective_id=0, has_side_effects=True, vmem_limit_bytes=60 * 1024 * 1024
        ),
    )(residue_mask, pair_act, *weights)


def solution(mesh):
    return jax.shard_map(
        shards,
        mesh=mesh,
        in_specs=(P("row", "col", None), P(), P(), P(), P(), P()),
        out_specs=P("row", "col", None),
        check_vma=False,
    )
```
